128 devices in a mesh: dp: 16 (over x, z_hi, core), mp: 8 (over y, z_lo).
Axes of the slice: x: 4, y: 4, z: 4 (z_hi: 2, z_lo: 2; z = z_hi * 2 + z_lo), core: 2. Of those that a mesh axis runs over, the one named last changes fastest.
Arguments:
- adapter_inputs: bfloat16 [49152, 64], P('dp'), may hold values from -6 to 6
- out_grads: bfloat16 [49152, 8192], P('dp', 'mp'), may hold values from -6 to 6
- routes: int32 [49152], P('dp'), may hold values from 0 to 1
- input_eigen_basis: float32 [2, 64, 64], replicated, may hold values from -0.75 to 0.75
- output_eigen_basis: bfloat16 [8192, 8192], P(None, 'mp'), may hold values from -0.0625 to 0.0625
- eigen_values: float32 [2, 64, 8192], P(None, None, 'mp'), may hold values from 0.05 to 1
- query_grads: bfloat16 [96, 2, 64, 8192], P('dp', None, None, 'mp'), may hold values from -6 to 6
Outputs:
- scores: float32 [48, 96], P('dp')
The draws below stay inside these ranges and needn't reach their ends.
All inputs are finite; a program needn't handle non-finite values.
Results may differ from the reference program's by a relative error of at most 0.0048.
Values may be sent and summed in bfloat16 or wider, within the bound.
A program may use at most 256 MiB of HBM per device.

```python
import math
import jax
import jax.numpy as jnp
from jax import lax

D = 8192
RANK = 64
EXPERTS = 2
LEN = 1024
SEQS = 48
QUERIES = 96
TRAIN_TOKENS = 49152


def set_ends(entries, rng, low, largest):
    index_at = [jax.random.randint(jax.random.fold_in(rng, axis), (), 0, length) for axis, length in enumerate(entries.shape)]
    widest = entries.shape.index(max(entries.shape))
    next_to = index_at[:widest] + [(index_at[widest] + 1) % entries.shape[widest]] + index_at[widest + 1:]
    return entries.at[tuple(index_at)].set(low).at[tuple(next_to)].set(largest)


def level_of(rng, shape, cuts, smallest, largest):
    level, own = 1.0, jax.random.fold_in(rng, 6)
    for dim, parts in cuts:
        draws = jnp.exp(jax.random.uniform(jax.random.fold_in(own, dim), (parts,), jnp.float32, smallest / len(cuts), largest / len(cuts)))
        level = level * jnp.repeat(draws, shape[dim] // parts).reshape([-1 if axis == dim else 1 for axis in range(len(shape))])
    return level


def noise(stream_key, shape, deviation, most, cuts=(), kind=jnp.bfloat16):
    level = level_of(stream_key, shape, cuts, -0.22, 0.18) if cuts else 1.0
    result = jax.random.normal(stream_key, shape, jnp.float32) * deviation * level
    return jnp.minimum(jnp.maximum(result, -most), most).astype(kind)


def setup_inputs(seed: int = 0) -> dict:
    key_of = jax.random.split(jax.random.key(seed), 8)
    adapter_inputs = noise(key_of[0], (TRAIN_TOKENS, RANK), 1.0, 6.0, ((0, 16),))
    out_grads = noise(key_of[1], (TRAIN_TOKENS, D), 1.0, 6.0, ((0, 16), (1, 8)))
    routes = set_ends(jax.random.randint(key_of[2], (TRAIN_TOKENS,), 0, EXPERTS), jax.random.fold_in(key_of[2], 1), 0, EXPERTS - 1).astype(jnp.int32)
    input_eigen_basis = noise(key_of[3], (EXPERTS, RANK, RANK), RANK ** -0.5, 0.75, (), jnp.float32)
    output_eigen_basis = noise(key_of[4], (D, D), D ** -0.5, 0.0625, ((1, 8),))
    eigen_values = jnp.clip(jnp.exp(math.log(1.0) - 2.9957323 * jax.random.uniform(key_of[5], (EXPERTS, RANK, D), jnp.float32) ** level_of(key_of[5], (EXPERTS, RANK, D), ((2, 8),), -0.2, 0.2)), 0.05, 1.0)
    query_grads = noise(key_of[6], (QUERIES, EXPERTS, RANK, D), 1.0, 6.0, ((0, 16), (3, 8)))
    return dict(adapter_inputs=adapter_inputs, out_grads=out_grads, routes=routes, input_eigen_basis=input_eigen_basis, output_eigen_basis=output_eigen_basis, eigen_values=eigen_values, query_grads=query_grads)


damping = 0.1

def reference(adapter_inputs, out_grads, routes, input_eigen_basis, output_eigen_basis, eigen_values, query_grads):
    spread = jnp.einsum('tr,ers->tes', adapter_inputs.astype(jnp.float32), input_eigen_basis, precision=lax.Precision.HIGHEST)
    picked_option = routes[:, None] == jnp.arange(EXPERTS, dtype=jnp.int32)[None, :]
    input_rotated_rows = jnp.where(picked_option[:, :, None], spread, 0.0).astype(jnp.bfloat16)
    input_rotated_rows = input_rotated_rows.reshape(SEQS, LEN, EXPERTS * RANK)
    sequence_gradients = out_grads.reshape(SEQS, LEN, D)
    unrotated_gradients = jnp.einsum('tnh,tnj->thj', input_rotated_rows.astype(jnp.float32), sequence_gradients.astype(jnp.float32)).astype(jnp.bfloat16)
    training_gradients = jnp.dot(unrotated_gradients.reshape(SEQS * EXPERTS * RANK, D), output_eigen_basis, preferred_element_type=jnp.float32).astype(jnp.bfloat16)
    train_flat = training_gradients.reshape(SEQS, EXPERTS * RANK * D).astype(jnp.float32)
    precond = (query_grads.astype(jnp.float32) / (eigen_values + damping)[None]).reshape(QUERIES, EXPERTS * RANK * D)
    scale = 1.0 / jnp.sqrt(jnp.float32(LEN * EXPERTS * RANK * D))
    return jnp.dot(train_flat, precond.T, precision=lax.Precision.HIGHEST) * scale
```

```python
import functools
import math

import jax
import jax.numpy as jnp
from jax import lax
from jax.experimental import pallas as pl
from jax.experimental.pallas import tpu as pltpu
from jax.sharding import PartitionSpec as P

LEN = 1024
LANES = 128
DAMPING = 0.1
F32, BF16 = jnp.float32, jnp.bfloat16

GROUPS = 8
CORES = 2
YS = 4
NT = (((1,), (1,)), ((), ()))


def kernel(
    dims,
    a_ref, routes_ref, basis_ref, g_hbm, u_hbm, eig_hbm, q_hbm,
    out_ref,
    g_v, u_v, eig_v, raw, gat, qbuf, qwide, qrow, acc, part, got, mine, all_mine,
    g_sem, u_sem, l_sem,
    a_send, a_recv, z_send, z_recv, y_send, y_recv, f_send, f_recv,
    q_send, q_recv, c_send, c_recv, r_send, r_recv, t_send, t_recv,
):
    seqs, rows, rank, experts, width, queries, blk = dims
    piece = seqs * blk
    dp, mp = lax.axis_index("dp"), lax.axis_index("mp")
    s, k = dp // CORES, dp % CORES
    y, l = mp // 2, mp % 2

    def dp_peer(b):
        return {"dp": b * CORES + k, "mp": mp}

    def mp_peer(m):
        return {"dp": dp, "mp": m}

    def at(dy, dl):
        return ((y + dy) % YS) * 2 + (l + dl) % 2

    def remote(src, dst, send, recv, dev):
        return pltpu.make_async_remote_copy(
            src_ref=src, dst_ref=dst, send_sem=send, recv_sem=recv, device_id=dev
        )

    def src_of(o):
        return (s + GROUPS - o) % GROUPS

    for n in range(seqs):
        pltpu.make_async_copy(g_hbm.at[n], g_v.at[n], g_sem.at[n]).start()
    eig_copy = pltpu.make_async_copy(
        eig_hbm.at[pl.ds(pl.multiple_of(s * blk, blk), blk), :], eig_v, l_sem.at[0]
    )
    eig_copy.start()

    barrier = pltpu.get_barrier_semaphore()
    for o in range(1, GROUPS):
        pl.semaphore_signal(barrier, inc=1, device_id=dp_peer((s + o) % GROUPS))
        pl.semaphore_signal(barrier, inc=1, device_id=mp_peer((mp + o) % GROUPS))
    partner = {"dp": s * CORES + 1 - k, "mp": mp}
    pl.semaphore_signal(barrier, inc=1, device_id=partner)

    for m in range(GROUPS):
        pltpu.make_async_copy(u_hbm.at[m], u_v.at[m], u_sem.at[m]).start()

    basis = basis_ref[...]
    parts, rest = [], basis
    for _ in range(3):
        parts.append(rest.astype(BF16))
        rest = rest - parts[-1].astype(F32)
    row_expert = lax.broadcasted_iota(jnp.int32, (rows, 1), 0) // rank

    def sequence(n, carry):
        pltpu.make_async_copy(g_hbm.at[n], g_v.at[n], g_sem.at[n]).wait()
        a = a_ref[n]
        spread = lax.dot_general(parts[2], a, NT, preferred_element_type=F32)
        spread += lax.dot_general(parts[1], a, NT, preferred_element_type=F32)
        spread += lax.dot_general(parts[0], a, NT, preferred_element_type=F32)
        rotated = jnp.where(routes_ref[n] == row_expert, spread, 0.0).astype(BF16)
        sums = jnp.dot(rotated, g_v[n], preferred_element_type=F32).astype(BF16)
        raw[:, pl.ds(pl.multiple_of(n * blk, blk), blk), :] = sums.reshape(GROUPS, blk, width)
        return carry

    lax.fori_loop(0, seqs, sequence, 0)
    gat[mp, s] = raw[s]

    pl.semaphore_wait(barrier, 2 * (GROUPS - 1) + 1)

    def a_copy(o):
        b = (s + o) % GROUPS
        return remote(raw.at[b], gat.at[mp, s], a_send.at[o], a_recv.at[o], dp_peer(b))

    def y_copy(o, side, way):
        slot = gat.at[at(0, side), src_of(o)]
        return remote(
            slot, slot, y_send.at[side, way, o], y_recv.at[side, way, o],
            mp_peer(at(1 if way == 0 else YS - 1, 0)),
        )

    def y_landed(o, side, way):
        slot = gat.at[at(YS - 1 if way == 0 else 1, side), src_of(o)]
        return remote(
            slot, slot, y_send.at[side, way, o], y_recv.at[side, way, o],
            mp_peer(at(1 if way == 0 else YS - 1, 0)),
        )

    def f_copy(o, side, way):
        slot = gat.at[at(YS - 1 if way == 0 else 1, side), src_of(o)]
        return remote(
            slot, slot, f_send.at[side, o], f_recv.at[side, o],
            mp_peer(at(1 if way == 0 else YS - 1, 0)),
        )

    def f_landed(o, side):
        slot = gat.at[at(2, side), src_of(o)]
        return remote(slot, slot, f_send.at[side, o], f_recv.at[side, o], mp_peer(at(1, 0)))

    def z_copy(o):
        slot = gat.at[mp, src_of(o)]
        return remote(slot, slot, z_send.at[o], z_recv.at[o], mp_peer(at(0, 1)))

    def z_landed(o):
        slot = gat.at[at(0, 1), src_of(o)]
        return remote(slot, slot, z_send.at[o], z_recv.at[o], mp_peer(at(0, 1)))

    def a_landed(o):
        slot = gat.at[mp, src_of(o)]
        return remote(slot, slot, a_send.at[o], a_recv.at[o], dp_peer(src_of(o)))

    def q_source(b):
        return q_hbm.at[:, pl.ds(pl.multiple_of(b * blk, blk), blk), :]

    def q_copy(o):
        b = (s + o) % GROUPS
        return remote(q_source(b), qbuf.at[s, k], q_send.at[o], q_recv.at[o], dp_peer(b))

    def q_landed(o):
        slot = qbuf.at[src_of(o), k]
        return remote(slot, slot, q_send.at[o], q_recv.at[o], dp_peer(src_of(o)))

    def send_own(o):
        z_copy(o).start()
        y_copy(o, 0, 0).start()
        y_copy(o, 0, 1).start()

    def each(low, high, body):
        def run(o, carry):
            body(o)
            return carry

        lax.fori_loop(low, high, run, 0)

    each(1, GROUPS, lambda o: a_copy(o).start())
    send_own(0)

    def arrived(o):
        a_landed(o).wait_recv()
        send_own(o)

    each(1, GROUPS, arrived)

    q_own = pltpu.make_async_copy(q_source(s), qbuf.at[s, k], l_sem.at[1])
    q_own.start()
    each(1, GROUPS, lambda o: q_copy(o).start())

    def multiply(m, first):
        pltpu.make_async_copy(u_hbm.at[m], u_v.at[m], u_sem.at[m]).wait()
        step = 256

        def column(i, carry):
            cols = pl.ds(pl.multiple_of(i * step, step), step)
            product = jnp.dot(
                gat[m].reshape(GROUPS * piece, width), u_v[m, :, cols],
                preferred_element_type=F32,
            )
            for half in range(step // LANES):
                lanes = i * (step // LANES) + half
                term = product[:, half * LANES : (half + 1) * LANES]
                acc[lanes] = term if first else acc[lanes] + term
            return carry

        lax.fori_loop(0, width // step, column, 0)

    multiply(mp, True)

    def forward_even(o, side):
        y_landed(o, side, 0).wait_recv()
        f_copy(o, side, 0).start()

    def forward_odd(o, side):
        y_landed(o, side, 1).wait_recv()
        f_copy(o, side, 1).start()

    def pair(i):
        for o in (2 * i, 2 * i + 1):
            z_landed(o).wait_recv()
            y_copy(o, 1, 0).start()
            y_copy(o, 1, 1).start()
        forward_even(2 * i, 0)
        forward_odd(2 * i + 1, 0)

    each(0, GROUPS // 2, pair)
    multiply(at(0, 1), False)

    def rest_of(side):
        def body(i):
            y_landed(2 * i, side, 1).wait_recv()
            y_landed(2 * i + 1, side, 0).wait_recv()
        return body

    each(0, GROUPS // 2, rest_of(0))
    multiply(at(1, 0), False)
    multiply(at(YS - 1, 0), False)

    each(1, GROUPS, lambda o: q_landed(o).wait_recv())
    q_own.wait()
    c_copy = remote(qbuf.at[:, k], qbuf.at[:, k], c_send.at[0], c_recv.at[0], partner)
    c_copy.start()

    def pair_far(i):
        forward_even(2 * i, 1)
        forward_odd(2 * i + 1, 1)

    each(0, GROUPS // 2, pair_far)

    remote(qbuf.at[:, 1 - k], qbuf.at[:, 1 - k], c_send.at[0], c_recv.at[0], partner).wait_recv()
    total = GROUPS * CORES * queries

    def widen(i, carry):
        chunk = queries * CORES * blk
        own = pl.ds(pl.multiple_of(i * chunk, chunk), chunk)
        for lanes in range(width // LANES):
            cols = qbuf[i, :, :, :, lanes * LANES : (lanes + 1) * LANES]
            qwide[lanes, own, :] = cols.reshape(chunk, LANES).astype(F32)
        return carry

    lax.fori_loop(0, GROUPS, widen, 0)

    def regroup(r, carry):
        for lanes in range(width // LANES):
            cols = qwide[lanes, pl.ds(r, total, stride=blk), :]
            qrow[r, :, lanes * LANES : (lanes + 1) * LANES] = cols.astype(BF16)
        return carry

    lax.fori_loop(0, blk, regroup, 0)
    eig_copy.wait()
    eig_v[...] = 1.0 / (eig_v[...] + DAMPING)

    each(0, GROUPS, lambda o: f_landed(o, 0).wait_recv())
    multiply(at(2, 0), False)
    each(0, GROUPS // 2, rest_of(1))
    multiply(at(1, 1), False)
    multiply(at(YS - 1, 1), False)
    each(0, GROUPS, lambda o: f_landed(o, 1).wait_recv())
    multiply(at(2, 1), False)

    count = GROUPS * seqs

    def score(r, carry):
        train = jnp.concatenate(
            [acc[lanes, pl.ds(r, count, stride=blk), :] for lanes in range(width // LANES)], axis=1
        )
        train = train.astype(BF16).astype(F32)
        train = train * eig_v[pl.ds(r, 1), :]
        high = train.astype(BF16)
        low = (train - high.astype(F32)).astype(BF16)
        carry += lax.dot_general(high, qrow[r], NT, preferred_element_type=F32)
        carry += lax.dot_general(low, qrow[r], NT, preferred_element_type=F32)
        return carry

    scores = lax.fori_loop(0, blk, score, jnp.zeros((count, total), F32))
    part[...] = jnp.zeros(part.shape, F32)
    for b in range(GROUPS):
        part[b, :seqs, :total] = scores[b * seqs : (b + 1) * seqs]

    def r_copy(o):
        b = (s + o) % GROUPS
        return remote(part.at[b], got.at[s], r_send.at[o], r_recv.at[o], dp_peer(b))

    def r_landed(o):
        slot = got.at[src_of(o)]
        return remote(slot, slot, r_send.at[o], r_recv.at[o], dp_peer(src_of(o)))

    each(1, GROUPS, lambda o: r_copy(o).start())
    got[s] = part[s]
    each(1, GROUPS, lambda o: r_landed(o).wait_recv())
    mine[...] = jnp.sum(got[...], axis=0)

    def t_copy(o):
        m = (mp + o) % GROUPS
        return remote(mine, all_mine.at[mp], t_send.at[o], t_recv.at[o], mp_peer(m))

    def t_landed(o):
        m = (mp + GROUPS - o) % GROUPS
        slot = all_mine.at[m]
        return remote(slot, slot, t_send.at[o], t_recv.at[o], mp_peer(m))

    each(1, GROUPS, lambda o: t_copy(o).start())
    all_mine[mp] = mine[...]
    each(1, GROUPS, lambda o: t_landed(o).wait_recv())
    result = jnp.sum(all_mine[...], axis=0)
    scale = 1.0 / math.sqrt(LEN * rows * width * GROUPS)
    out_ref[...] = result[:seqs, :total] * scale

    def sent(o):
        a_copy(o).wait_send()
        q_copy(o).wait_send()
        r_copy(o).wait_send()
        t_copy(o).wait_send()

    each(1, GROUPS, sent)

    def sent_pieces(o):
        z_copy(o).wait_send()
        for side in (0, 1):
            y_copy(o, side, 0).wait_send()
            y_copy(o, side, 1).wait_send()

    each(0, GROUPS, sent_pieces)

    def sent_forward(i):
        for side in (0, 1):
            f_copy(2 * i, side, 0).wait_send()
            f_copy(2 * i + 1, side, 1).wait_send()

    each(0, GROUPS // 2, sent_forward)
    c_copy.wait_send()


def local(adapter_inputs, out_grads, routes, input_eigen_basis, output_eigen_basis, eigen_values, query_grads):
    tokens, rank = adapter_inputs.shape
    experts = input_eigen_basis.shape[0]
    rows = experts * rank
    width = out_grads.shape[1]
    queries = query_grads.shape[0]
    seqs = tokens // LEN
    blk = rows // GROUPS
    dims = (seqs, rows, rank, experts, width, queries, blk)
    piece = seqs * blk
    total = GROUPS * CORES * queries
    vmem, hbm = pl.BlockSpec(memory_space=pltpu.VMEM), pl.BlockSpec(memory_space=pl.ANY)
    dma = pltpu.SemaphoreType.DMA
    return pl.pallas_call(
        functools.partial(kernel, dims),
        out_shape=jax.ShapeDtypeStruct((seqs, total), F32),
        in_specs=[vmem, vmem, vmem, hbm, hbm, hbm, hbm],
        out_specs=vmem,
        scratch_shapes=[
            pltpu.VMEM((seqs, LEN, width), BF16),
            pltpu.VMEM((GROUPS, width, width), BF16),
            pltpu.VMEM((blk, width), F32),
            pltpu.VMEM((GROUPS, piece, width), BF16),
            pltpu.VMEM((GROUPS, GROUPS, piece, width), BF16),
            pltpu.VMEM((GROUPS, CORES, queries, blk, width), BF16),
            pltpu.VMEM((width // LANES, total * blk, LANES), F32),
            pltpu.VMEM((blk, total, width), BF16),
            pltpu.VMEM((width // LANES, GROUPS * piece, LANES), F32),
            pltpu.VMEM((GROUPS, 8, 128), F32),
            pltpu.VMEM((GROUPS, 8, 128), F32),
            pltpu.VMEM((8, 128), F32),
            pltpu.VMEM((GROUPS, 8, 128), F32),
            dma((seqs,)), dma((GROUPS,)), dma((2,)),
            dma((GROUPS,)), dma((GROUPS,)), dma((GROUPS,)), dma((GROUPS,)),
            dma((2, 2, GROUPS)), dma((2, 2, GROUPS)), dma((2, GROUPS)), dma((2, GROUPS)),
            dma((GROUPS,)), dma((GROUPS,)), dma((1,)), dma((1,)),
            dma((GROUPS,)), dma((GROUPS,)), dma((GROUPS,)), dma((GROUPS,)),
        ],
        compiler_params=pltpu.CompilerParams(
            collective_id=0, has_side_effects=True, vmem_limit_bytes=58 * 2**20
        ),
    )(
        adapter_inputs.reshape(seqs, LEN, rank),
        routes.reshape(seqs, 1, LEN),
        input_eigen_basis.transpose(0, 2, 1).reshape(rows, rank),
        out_grads.reshape(seqs, LEN, width),
        output_eigen_basis.reshape(GROUPS, width, width),
        eigen_values.reshape(rows, width),
        query_grads.reshape(queries, rows, width),
    )


def solution(mesh):
    placed = (
        P("dp", None),
        P("dp", "mp"),
        P("dp"),
        P(),
        P(None, "mp"),
        P(None, None, "mp"),
        P("dp", None, None, "mp"),
    )
    return jax.shard_map(
        local, mesh=mesh, in_specs=placed, out_specs=P("dp", None), check_vma=False
    )
```

```python
import functools
import math

import jax
import jax.numpy as jnp
from jax import lax
from jax.experimental import pallas as pl
from jax.experimental.pallas import tpu as pltpu
from jax.sharding import PartitionSpec as P

LEN = 1024
LANES = 128
DAMPING = 0.1
F32, BF16 = jnp.float32, jnp.bfloat16

GROUPS = 8
CORES = 2
YS = 4
ORDER = (0, 1, 7, 2, 6, 3, 5, 4)
EARLY = (0, 1)
NT = (((1,), (1,)), ((), ()))


def kernel(
    dims,
    a_ref, routes_ref, basis_ref, g_hbm, u_hbm, eig_hbm, q_hbm,
    out_ref,
    g_v, u_v, eig_v, raw, gat, qbuf, qwide, qrow, acc, part, got,
    g_sem, u_sem, l_sem,
    a_send, a_recv, z_send, z_recv, e_send, e_recv, y_send, y_recv, f_send, f_recv,
    q_send, q_recv, c_send, c_recv, r_send, r_recv,
):
    seqs, rows, rank, experts, width, queries, blk = dims
    piece = seqs * blk
    dp, mp = lax.axis_index("dp"), lax.axis_index("mp")
    s, k = dp // CORES, dp % CORES
    y, l = mp // 2, mp % 2

    def dp_peer(b):
        return {"dp": b * CORES + k, "mp": mp}

    def mp_peer(m):
        return {"dp": dp, "mp": m}

    def at(dy, dl):
        return ((y + dy) % YS) * 2 + (l + dl) % 2

    def remote(src, dst, send, recv, dev):
        return pltpu.make_async_remote_copy(
            src_ref=src, dst_ref=dst, send_sem=send, recv_sem=recv, device_id=dev
        )

    partner = {"dp": s * CORES + 1 - k, "mp": mp}

    for n in range(seqs):
        pltpu.make_async_copy(g_hbm.at[n], g_v.at[n], g_sem.at[n]).start()
    eig_copy = pltpu.make_async_copy(
        eig_hbm.at[pl.ds(pl.multiple_of(s * blk, blk), blk), :], eig_v, l_sem.at[0]
    )
    eig_copy.start()

    barrier = pltpu.get_barrier_semaphore()
    greeted = [dp_peer((s + o) % GROUPS) for o in range(1, GROUPS)]
    greeted += [
        {"dp": (s + o) % GROUPS * CORES + k, "mp": at(0, 1)} for o in range(1, GROUPS, 2)
    ]
    greeted += [mp_peer(at(1, 0)), mp_peer(at(YS - 1, 0)), mp_peer(at(0, 1)), partner]
    for device in greeted:
        pl.semaphore_signal(barrier, inc=1, device_id=device)

    for m in range(GROUPS):
        pltpu.make_async_copy(u_hbm.at[m], u_v.at[m], u_sem.at[m]).start()

    basis = jnp.concatenate([basis_ref[e] for e in range(experts)], axis=1).T
    parts, rest = [], basis
    for _ in range(3):
        parts.append(rest.astype(BF16))
        rest = rest - parts[-1].astype(F32)
    row_expert = lax.broadcasted_iota(jnp.int32, (rows, 1), 0) // rank

    def sequence(n, carry):
        pltpu.make_async_copy(g_hbm.at[n], g_v.at[n], g_sem.at[n]).wait()
        a = a_ref[:, pl.ds(pl.multiple_of(n * LEN, LEN), LEN)]
        spread = jnp.dot(parts[2], a, preferred_element_type=F32)
        spread += jnp.dot(parts[1], a, preferred_element_type=F32)
        spread += jnp.dot(parts[0], a, preferred_element_type=F32)
        rotated = jnp.where(routes_ref[n] == row_expert, spread, 0.0).astype(BF16)
        sums = jnp.dot(rotated, g_v[n], preferred_element_type=F32).astype(BF16)
        raw[:, pl.ds(pl.multiple_of(n * blk, blk), blk), :] = sums.reshape(GROUPS, blk, width)
        return carry

    lax.fori_loop(0, seqs, sequence, 0)
    gat[mp, 0] = raw[s]

    pl.semaphore_wait(barrier, len(greeted))

    first_col = [o % 2 for o in ORDER]
    direct = [i for i in range(GROUPS) if i not in EARLY]
    f_way = {(i, first_col[i]): i % 2 for i in range(GROUPS)}
    f_way.update({(i, 1 - first_col[i]): n % 2 for n, i in enumerate(direct)})

    def slot(dy, col, i):
        return gat.at[at(dy % YS, col), i]

    def a_copy(i):
        b = (s + ORDER[i]) % GROUPS
        device = {"dp": b * CORES + k, "mp": at(0, first_col[i])}
        return remote(raw.at[b], gat.at[mp, i], a_send.at[i], a_recv.at[i], device)

    def a_landed(i):
        here = slot(0, first_col[i], i)
        return remote(here, here, a_send.at[i], a_recv.at[i], partner)

    def z_copy(i):
        here = slot(0, first_col[i], i)
        return remote(here, here, z_send.at[i], z_recv.at[i], mp_peer(at(0, 1)))

    def z_landed(i):
        here = slot(0, 1 - first_col[i], i)
        return remote(here, here, z_send.at[i], z_recv.at[i], mp_peer(at(0, 1)))

    def way_peer(way):
        return mp_peer(at(1 if way == 0 else YS - 1, 0))

    def y_copy(i, col, way):
        here = slot(0, col, i)
        return remote(here, here, y_send.at[col, way, i], y_recv.at[col, way, i], way_peer(way))

    def y_landed(i, col, way):
        here = slot(-1 if way == 0 else 1, col, i)
        return remote(here, here, y_send.at[col, way, i], y_recv.at[col, way, i], way_peer(way))

    def f_copy(i, col):
        way = f_way[i, col]
        here = slot(-1 if way == 0 else 1, col, i)
        return remote(here, here, f_send.at[col, i], f_recv.at[col, i], way_peer(way))

    def f_landed(i, col):
        here = slot(2, col, i)
        return remote(here, here, f_send.at[col, i], f_recv.at[col, i], partner)

    def e_copy(i, dy):
        here = slot(dy, first_col[i], i)
        n = EARLY.index(i)
        return remote(here, here, e_send.at[n, dy % YS], e_recv.at[n, dy % YS], mp_peer(at(0, 1)))

    def e_landed(i, dy):
        here = slot(dy, 1 - first_col[i], i)
        n = EARLY.index(i)
        return remote(here, here, e_send.at[n, dy % YS], e_recv.at[n, dy % YS], partner)

    def q_source(b):
        return q_hbm.at[:, pl.ds(pl.multiple_of(b * blk, blk), blk), :]

    def q_copy(i):
        b = (s + ORDER[i]) % GROUPS
        return remote(q_source(b), qbuf.at[s, k], q_send.at[i], q_recv.at[i], dp_peer(b))

    def q_landed(i):
        here = qbuf.at[(s + GROUPS - ORDER[i]) % GROUPS, k]
        return remote(here, here, q_send.at[i], q_recv.at[i], partner)

    def both_ways(i, col):
        y_copy(i, col, 0).start()
        y_copy(i, col, 1).start()

    def forward(i, col):
        y_landed(i, col, f_way[i, col]).wait_recv()
        f_copy(i, col).start()

    def other_way(i, col):
        y_landed(i, col, 1 - f_way[i, col]).wait_recv()

    def multiply(m, low=0, high=GROUPS, first=False, wait=True):
        if wait:
            pltpu.make_async_copy(u_hbm.at[m], u_v.at[m], u_sem.at[m]).wait()
        step = 256

        def column(c, carry):
            cols = pl.ds(pl.multiple_of(c * step, step), step)
            product = jnp.dot(
                gat[m, low:high].reshape((high - low) * piece, width), u_v[m, :, cols],
                preferred_element_type=F32,
            )
            own = slice(low * piece, high * piece)
            for half in range(step // LANES):
                lanes = c * (step // LANES) + half
                term = product[:, half * LANES : (half + 1) * LANES]
                acc[lanes, own] = term if first else acc[lanes, own] + term
            return carry

        lax.fori_loop(0, width // step, column, 0)

    for i in range(1, GROUPS):
        a_copy(i).start()
    for i in range(GROUPS):
        if i:
            a_landed(i).wait_recv()
        both_ways(i, first_col[i])
        z_copy(i).start()

    q_own = pltpu.make_async_copy(q_source(s), qbuf.at[s, k], l_sem.at[1])
    q_own.start()
    for i in range(1, GROUPS):
        q_copy(i).start()

    for i in range(GROUPS):
        forward(i, first_col[i])
        if i in EARLY:
            other_way(i, first_col[i])
            e_copy(i, 1).start()
            e_copy(i, -1).start()
        z_landed(i).wait_recv()
        if i in direct:
            both_ways(i, 1 - first_col[i])
    multiply(at(0, 0), first=True)
    for i in EARLY:
        f_landed(i, first_col[i]).wait_recv()
        e_copy(i, 2).start()
    multiply(at(0, 1))
    for i in direct[: len(direct) // 2]:
        forward(i, 1 - first_col[i])

    for i in range(1, GROUPS):
        q_landed(i).wait_recv()
    q_own.wait()
    c_copy = remote(qbuf.at[:, k], qbuf.at[:, k], c_send.at[0], c_recv.at[0], partner)
    c_copy.start()
    for i in direct[len(direct) // 2 :]:
        forward(i, 1 - first_col[i])
    remote(qbuf.at[:, 1 - k], qbuf.at[:, 1 - k], c_send.at[0], c_recv.at[0], partner).wait_recv()
    total = GROUPS * CORES * queries

    def widen(g, carry):
        chunk = queries * CORES * blk
        own = pl.ds(pl.multiple_of(g * chunk, chunk), chunk)
        for lanes in range(width // LANES):
            cols = qbuf[g, :, :, :, lanes * LANES : (lanes + 1) * LANES]
            qwide[lanes, own, :] = cols.reshape(chunk, LANES).astype(F32)
        return carry

    lax.fori_loop(0, GROUPS, widen, 0)

    def regroup(r, carry):
        for lanes in range(width // LANES):
            cols = qwide[lanes, pl.ds(r, total, stride=blk), :]
            qrow[r, :, lanes * LANES : (lanes + 1) * LANES] = cols.astype(BF16)
        return carry

    lax.fori_loop(0, blk, regroup, 0)
    eig_copy.wait()
    eig_v[...] = 1.0 / (eig_v[...] + DAMPING)

    for i in range(GROUPS):
        if i not in EARLY:
            other_way(i, first_col[i])
    for i in direct:
        other_way(i, 1 - first_col[i])
    for i in EARLY:
        e_landed(i, 1).wait_recv()
        e_landed(i, -1).wait_recv()
    for dy in (1, -1):
        for col in (0, 1):
            multiply(at(dy % YS, col))

    def far(i):
        if i not in EARLY:
            f_landed(i, first_col[i]).wait_recv()
        if i in direct:
            f_landed(i, 1 - first_col[i]).wait_recv()
        else:
            e_landed(i, 2).wait_recv()

    def score(low, high):
        count = (high - low) * seqs
        scores = jnp.zeros((count, total), F32)
        for r in range(blk):
            own = pl.ds(low * piece + r, count, stride=blk)
            train = jnp.concatenate([acc[lanes, own, :] for lanes in range(width // LANES)], axis=1)
            train = train.astype(BF16).astype(F32) * eig_v[r : r + 1, :]
            upper = train.astype(BF16)
            lower = (train - upper.astype(F32)).astype(BF16)
            scores += lax.dot_general(upper, qrow[r], NT, preferred_element_type=F32)
            scores += lax.dot_general(lower, qrow[r], NT, preferred_element_type=F32)
        for i in range(low, high):
            part[i, :seqs, :total] = scores[(i - low) * seqs : (i - low + 1) * seqs]

    part[...] = jnp.zeros(part.shape, F32)
    half = GROUPS // 2
    for low in (0, half):
        for i in range(low, low + half):
            far(i)
        for col in (0, 1):
            multiply(at(2, col), low, low + half, wait=low == 0)
        score(low, low + half)

    me = s * GROUPS + mp

    def r_copy(i, m):
        device = {"dp": (s + GROUPS - ORDER[i]) % GROUPS * CORES + k, "mp": m}
        return remote(part.at[i], got.at[me], r_send.at[0], r_recv.at[0], device)

    for i in range(1, GROUPS):
        r_copy(i, mp).start()

    def round_mp(o, carry):
        for i in range(GROUPS):
            r_copy(i, (mp + o) % GROUPS).start()
        return carry

    lax.fori_loop(1, GROUPS, round_mp, 0)
    got[me] = part[0]
    others = got.at[pl.ds(0, GROUPS * GROUPS - 1)]
    r_all = remote(others, others, r_send.at[0], r_recv.at[0], partner)
    r_all.wait_recv()
    scale = 1.0 / math.sqrt(LEN * rows * width * GROUPS)
    out_ref[...] = jnp.sum(got[...], axis=0)[:seqs, :total] * scale

    r_all.wait_send()
    c_copy.wait_send()
    for i in range(GROUPS):
        if i:
            a_copy(i).wait_send()
            q_copy(i).wait_send()
        z_copy(i).wait_send()
        if i in EARLY:
            for dy in (1, -1, 2):
                e_copy(i, dy).wait_send()
        for col in (0, 1):
            if (i, col) in f_way:
                y_copy(i, col, 0).wait_send()
                y_copy(i, col, 1).wait_send()
                f_copy(i, col).wait_send()


def local(adapter_inputs, out_grads, routes, input_eigen_basis, output_eigen_basis, eigen_values, query_grads):
    tokens, rank = adapter_inputs.shape
    experts = input_eigen_basis.shape[0]
    rows = experts * rank
    width = out_grads.shape[1]
    queries = query_grads.shape[0]
    seqs = tokens // LEN
    blk = rows // GROUPS
    dims = (seqs, rows, rank, experts, width, queries, blk)
    piece = seqs * blk
    total = GROUPS * CORES * queries
    vmem, hbm = pl.BlockSpec(memory_space=pltpu.VMEM), pl.BlockSpec(memory_space=pl.ANY)
    dma = pltpu.SemaphoreType.DMA
    return pl.pallas_call(
        functools.partial(kernel, dims),
        out_shape=jax.ShapeDtypeStruct((seqs, total), F32),
        in_specs=[vmem, vmem, vmem, hbm, hbm, hbm, hbm],
        out_specs=vmem,
        scratch_shapes=[
            pltpu.VMEM((seqs, LEN, width), BF16),
            pltpu.VMEM((GROUPS, width, width), BF16),
            pltpu.VMEM((blk, width), F32),
            pltpu.VMEM((GROUPS, piece, width), BF16),
            pltpu.VMEM((GROUPS, GROUPS, piece, width), BF16),
            pltpu.VMEM((GROUPS, CORES, queries, blk, width), BF16),
            pltpu.VMEM((width // LANES, total * blk, LANES), F32),
            pltpu.VMEM((blk, total, width), BF16),
            pltpu.VMEM((width // LANES, GROUPS * piece, LANES), F32),
            pltpu.VMEM((GROUPS, 4, LANES), F32),
            pltpu.VMEM((GROUPS * GROUPS, 4, LANES), F32),
            dma((seqs,)), dma((GROUPS,)), dma((2,)),
            dma((GROUPS,)), dma((GROUPS,)), dma((GROUPS,)), dma((GROUPS,)),
            dma((len(EARLY), YS)), dma((len(EARLY), YS)),
            dma((2, 2, GROUPS)), dma((2, 2, GROUPS)), dma((2, GROUPS)), dma((2, GROUPS)),
            dma((GROUPS,)), dma((GROUPS,)), dma((1,)), dma((1,)), dma((1,)), dma((1,)),
        ],
        compiler_params=pltpu.CompilerParams(
            collective_id=0, has_side_effects=True, vmem_limit_bytes=58 * 2**20
        ),
    )(
        adapter_inputs.T,
        routes.reshape(seqs, 1, LEN),
        input_eigen_basis,
        out_grads.reshape(seqs, LEN, width),
        output_eigen_basis.reshape(GROUPS, width, width),
        eigen_values.reshape(rows, width),
        query_grads.reshape(queries, rows, width),
    )


def solution(mesh):
    placed = (
        P("dp", None),
        P("dp", "mp"),
        P("dp"),
        P(),
        P(None, "mp"),
        P(None, None, "mp"),
        P("dp", None, None, "mp"),
    )
    return jax.shard_map(
        local, mesh=mesh, in_specs=placed, out_specs=P("dp", None), check_vma=False
    )
```

```python
import functools
import math

import jax
import jax.numpy as jnp
from jax import lax
from jax.experimental import pallas as pl
from jax.experimental.pallas import tpu as pltpu
from jax.sharding import PartitionSpec as P

LEN = 1024
LANES = 128
DAMPING = 0.1
F32, BF16 = jnp.float32, jnp.bfloat16

GROUPS = 8
CORES = 2
YS = 4
ORDER = (0, 1, 7, 2, 6, 3, 5, 4)
EARLY = (3, 6)
SPLIT = 4
STEPS = (
    ("F", 0, 0), ("Z", 0), ("A", 1), ("A", 3), ("A", 4), ("A", 2), ("Z", 1), ("A", 5), ("F", 0, 1), ("A", 7),
    ("F", 1, 0), ("A", 6), ("Q", 1), ("Q", 2), ("Q", 7), ("Q", 5), ("Q", 6), ("Q", 4), ("Q", 3), ("F", 3, 0), ("E", 3, 1),
    ("Z", 4), ("E", 3, 0), ("Z", 2), ("M", 0, 0), ("F", 4, 0), ("Z", 5), ("F", 2, 0), ("F", 1, 1), ("F", 5, 0),
    ("F", 7, 0), ("Z", 7), ("E", 6, 1), ("F", 6, 0), ("E", 6, 0), ("G", 3), ("F", 4, 1), ("F", 2, 1), ("C",),
    ("M", 1, 0), ("F", 5, 1), ("M", 0, 2), ("M", 0, 1), ("R",), ("M", 1, 1), ("G", 6), ("F", 7, 1), ("M", 1, 2),
    ("M", 0, 3), ("M", 1, 3),
)
NT = (((1,), (1,)), ((), ()))


def kernel(
    dims,
    a_ref, routes_ref, basis_ref, g_hbm, u_hbm, eig_hbm, q_hbm,
    out_ref,
    g_v, u_v, eig_v, raw, gat, qbuf, qwide, qrow, acc, part, got,
    g_sem, u_sem, l_sem,
    a_send, a_recv, z_send, z_recv, e_send, e_recv, y_send, y_recv, f_send, f_recv,
    q_send, q_recv, c_send, c_recv, r_send, r_recv,
):
    seqs, rows, rank, experts, width, queries, blk = dims
    piece = seqs * blk
    dp, mp = lax.axis_index("dp"), lax.axis_index("mp")
    s, k = dp // CORES, dp % CORES
    y, l = mp // 2, mp % 2

    def dp_peer(b):
        return {"dp": b * CORES + k, "mp": mp}

    def mp_peer(m):
        return {"dp": dp, "mp": m}

    def at(dy, dl):
        return ((y + dy) % YS) * 2 + (l + dl) % 2

    def remote(src, dst, send, recv, dev):
        return pltpu.make_async_remote_copy(
            src_ref=src, dst_ref=dst, send_sem=send, recv_sem=recv, device_id=dev
        )

    partner = {"dp": s * CORES + 1 - k, "mp": mp}

    for n in range(seqs):
        pltpu.make_async_copy(g_hbm.at[n], g_v.at[n], g_sem.at[n]).start()
    eig_copy = pltpu.make_async_copy(
        eig_hbm.at[pl.ds(pl.multiple_of(s * blk, blk), blk), :], eig_v, l_sem.at[0]
    )
    eig_copy.start()

    barrier = pltpu.get_barrier_semaphore()
    greeted = [dp_peer((s + o) % GROUPS) for o in range(1, GROUPS)]
    greeted += [
        {"dp": (s + o) % GROUPS * CORES + k, "mp": at(0, 1)} for o in range(1, GROUPS, 2)
    ]
    greeted += [mp_peer(at(1, 0)), mp_peer(at(YS - 1, 0)), mp_peer(at(0, 1)), partner]
    for device in greeted:
        pl.semaphore_signal(barrier, inc=1, device_id=device)

    basis = jnp.concatenate([basis_ref[e] for e in range(experts)], axis=1).T
    parts, rest = [], basis
    for _ in range(3):
        parts.append(rest.astype(BF16))
        rest = rest - parts[-1].astype(F32)
    row_expert = lax.broadcasted_iota(jnp.int32, (rows, 1), 0) // rank

    def sequence(n):
        pltpu.make_async_copy(g_hbm.at[n], g_v.at[n], g_sem.at[n]).wait()
        a = a_ref[:, n * LEN : (n + 1) * LEN]
        spread = jnp.dot(parts[2], a, preferred_element_type=F32)
        spread += jnp.dot(parts[1], a, preferred_element_type=F32)
        spread += jnp.dot(parts[0], a, preferred_element_type=F32)
        rotated = jnp.where(routes_ref[n] == row_expert, spread, 0.0).astype(BF16)
        sums = jnp.dot(rotated, g_v[n], preferred_element_type=F32).astype(BF16)
        raw[:, n * blk : (n + 1) * blk, :] = sums.reshape(GROUPS, blk, width)

    first_col = [o % 2 for o in ORDER]
    direct = [i for i in range(GROUPS) if i not in EARLY]
    f_way = {(i, first_col[i]): i % 2 for i in range(GROUPS)}
    f_way.update({(i, 1 - first_col[i]): n % 2 for n, i in enumerate(direct)})

    def slot(dy, col, i):
        return gat.at[at(dy % YS, col), i]

    def a_copy(i, low=0, high=seqs):
        b = (s + ORDER[i]) % GROUPS
        device = {"dp": b * CORES + k, "mp": at(0, first_col[i])}
        own = pl.ds(low * blk, (high - low) * blk)
        return remote(raw.at[b, own], gat.at[mp, i, own], a_send.at[i], a_recv.at[i], device)

    def a_landed(i):
        here = slot(0, first_col[i], i)
        return remote(here, here, a_send.at[i], a_recv.at[i], partner)

    def z_copy(i, low=0, high=seqs):
        here = slot(0, first_col[i], i).at[pl.ds(low * blk, (high - low) * blk)]
        return remote(here, here, z_send.at[i], z_recv.at[i], mp_peer(at(0, 1)))

    def z_landed(i):
        here = slot(0, 1 - first_col[i], i)
        return remote(here, here, z_send.at[i], z_recv.at[i], mp_peer(at(0, 1)))

    def way_peer(way):
        return mp_peer(at(1 if way == 0 else YS - 1, 0))

    def y_copy(i, col, way, low=0, high=seqs):
        here = slot(0, col, i).at[pl.ds(low * blk, (high - low) * blk)]
        return remote(here, here, y_send.at[col, way, i], y_recv.at[col, way, i], way_peer(way))

    def y_landed(i, col, way):
        here = slot(-1 if way == 0 else 1, col, i)
        return remote(here, here, y_send.at[col, way, i], y_recv.at[col, way, i], way_peer(way))

    def f_copy(i, col):
        way = f_way[i, col]
        here = slot(-1 if way == 0 else 1, col, i)
        return remote(here, here, f_send.at[col, i], f_recv.at[col, i], way_peer(way))

    def f_landed(i, col):
        here = slot(2, col, i)
        return remote(here, here, f_send.at[col, i], f_recv.at[col, i], partner)

    def e_copy(i, dy):
        here = slot(dy, first_col[i], i)
        n = EARLY.index(i)
        return remote(here, here, e_send.at[n, dy % YS], e_recv.at[n, dy % YS], mp_peer(at(0, 1)))

    def e_landed(i, dy):
        here = slot(dy, 1 - first_col[i], i)
        n = EARLY.index(i)
        return remote(here, here, e_send.at[n, dy % YS], e_recv.at[n, dy % YS], partner)

    def q_source(b):
        return q_hbm.at[:, pl.ds(pl.multiple_of(b * blk, blk), blk), :]

    def q_copy(i):
        b = (s + ORDER[i]) % GROUPS
        return remote(q_source(b), qbuf.at[s, k], q_send.at[i], q_recv.at[i], dp_peer(b))

    def q_landed(i):
        here = qbuf.at[(s + GROUPS - ORDER[i]) % GROUPS, k]
        return remote(here, here, q_send.at[i], q_recv.at[i], partner)

    def both_ways(i, col):
        y_copy(i, col, 0).start()
        y_copy(i, col, 1).start()

    def forward(i, col):
        y_landed(i, col, f_way[i, col]).wait_recv()
        f_copy(i, col).start()

    def other_way(i, col):
        y_landed(i, col, 1 - f_way[i, col]).wait_recv()

    def multiply(dy, low, high, first, wait):
        def column(col, carry):
            m = at(dy, col)
            if wait:
                pltpu.make_async_copy(u_hbm.at[m], u_v.at[m], u_sem.at[m]).wait()
            product = jnp.dot(
                gat[m, low:high].reshape((high - low) * piece, width), u_v[m], preferred_element_type=F32
            )
            own = slice(low * piece, high * piece)
            for lanes in range(width // LANES):
                acc[lanes, own] += product[:, lanes * LANES : (lanes + 1) * LANES]
            return carry

        if first:
            acc[:, low * piece : high * piece] = jnp.zeros((width // LANES, (high - low) * piece, LANES), F32)
        lax.fori_loop(0, 2, column, 0)

    for n in range(seqs):
        sequence(n)
        if n == 0:
            pl.semaphore_wait(barrier, len(greeted))
        for i in range(1, GROUPS):
            a_copy(i, n, n + 1).start()
        gat[mp, 0, n * blk : (n + 1) * blk] = raw[s, n * blk : (n + 1) * blk]
        y_copy(0, first_col[0], 0, n, n + 1).start()
        y_copy(0, first_col[0], 1, n, n + 1).start()
        z_copy(0, n, n + 1).start()
    q_own = pltpu.make_async_copy(q_source(s), qbuf.at[s, k], l_sem.at[1])
    q_own.start()
    for m in range(GROUPS):
        pltpu.make_async_copy(u_hbm.at[m], u_v.at[m], u_sem.at[m]).start()
    acc[:, GROUPS * piece :] = jnp.zeros((width // LANES, blk * 4, LANES), F32)
    part[...] = jnp.zeros(part.shape, F32)
    eig_copy.wait()
    eig_v[...] = 1.0 / (eig_v[...] + DAMPING)
    c_copy = remote(qbuf.at[:, k], qbuf.at[:, k], c_send.at[0], c_recv.at[0], partner)
    c_here = remote(qbuf.at[:, 1 - k], qbuf.at[:, 1 - k], c_send.at[0], c_recv.at[0], partner)
    total = GROUPS * CORES * queries

    def widen(g, carry):
        chunk = queries * CORES * blk
        own = pl.ds(pl.multiple_of(g * chunk, chunk), chunk)
        for lanes in range(width // LANES):
            cols = qbuf[g, :, :, :, lanes * LANES : (lanes + 1) * LANES]
            qwide[lanes, own, :] = cols.reshape(chunk, LANES).astype(F32)
        return carry

    def regroup(r, carry):
        for lanes in range(width // LANES):
            cols = qwide[lanes, pl.ds(r, total, stride=blk), :]
            qrow[r, :, lanes * LANES : (lanes + 1) * LANES] = cols.astype(BF16)
        return carry

    def score(low, high):
        padded, step = 16, 4

        def some_rows(g, scores):
            for r in [g * step + n for n in range(step)]:
                own = pl.ds(low * piece + r, padded, stride=blk)
                train = jnp.concatenate([acc[lanes, own, :] for lanes in range(width // LANES)], axis=1)
                train = train.astype(BF16).astype(F32) * eig_v[pl.ds(r, 1), :]
                upper = train.astype(BF16).astype(F32)
                both = jnp.concatenate([upper, train - upper], axis=0).astype(BF16)
                scores += lax.dot_general(both, qrow[r], NT, preferred_element_type=F32)
            return scores

        scores = lax.fori_loop(0, blk // step, some_rows, jnp.zeros((2 * padded, total), F32))
        scores = scores[:padded] + scores[padded:]
        for i in range(low, high):
            part[i, :seqs, :total] = scores[(i - low) * seqs : (i - low + 1) * seqs]

    me = s * GROUPS + mp

    def r_copy(i, m):
        device = {"dp": (s + GROUPS - ORDER[i]) % GROUPS * CORES + k, "mp": m}
        return remote(part.at[i], got.at[me], r_send.at[0], r_recv.at[0], device)

    def send_scores(low, high):
        for o in (4, 5, 3, 2, 6, 1, 7, 0):
            for i in range(high - 1, low - 1, -1):
                if i or o:
                    r_copy(i, (mp + o) % GROUPS).start()

    waited, loaded = set(), set()

    def wait(copy, *name):
        if name not in waited:
            waited.add(name)
            copy(*name[1:]).wait_recv()

    def y_wait(i, second, way):
        wait(lambda *_: y_landed(i, first_col[i] ^ second, way), "y", i, second, way)

    def multiply_half(part_of, source):
        low, high = (0, SPLIT) if part_of == 0 else (SPLIT, GROUPS)
        dy = (0, -1, 1, 2)[source]
        for i in range(low, high):
            if source == 0:
                if i:
                    wait(a_landed, "a", i)
                wait(z_landed, "z", i)
            elif source == 3:
                wait(lambda *_: f_landed(i, first_col[i]), "f", i, 0)
                if i in EARLY:
                    e_landed(i, 2).wait_recv()
                else:
                    wait(lambda *_: f_landed(i, 1 - first_col[i]), "f", i, 1)
            else:
                y_wait(i, 0, source - 1)
                if i in EARLY:
                    e_landed(i, dy).wait_recv()
                else:
                    y_wait(i, 1, source - 1)
        multiply(dy % YS, low, high, source == 0, dy not in loaded)
        loaded.add(dy)
        if source == 3:
            score(low, high)
            send_scores(low, high)

    for step, *arg in STEPS:
        if step == "A":
            wait(a_landed, "a", arg[0])
            both_ways(arg[0], first_col[arg[0]])
            z_copy(arg[0]).start()
        elif step == "Z":
            wait(z_landed, "z", arg[0])
            both_ways(arg[0], 1 - first_col[arg[0]])
        elif step == "F":
            i, second = arg
            y_wait(i, second, f_way[i, first_col[i] ^ second])
            f_copy(i, first_col[i] ^ second).start()
        elif step == "E":
            i, way = arg
            y_wait(i, 0, way)
            e_copy(i, -1 if way == 0 else 1).start()
        elif step == "G":
            i = arg[0]
            wait(lambda *_: f_landed(i, first_col[i]), "f", i, 0)
            e_copy(i, 2).start()
        elif step == "Q":
            q_copy(arg[0]).start()
        elif step == "C":
            for i in range(1, GROUPS):
                q_landed(i).wait_recv()
            q_own.wait()
            c_copy.start()
        elif step == "R":
            c_here.wait_recv()
            lax.fori_loop(0, GROUPS, widen, 0)
            lax.fori_loop(0, blk, regroup, 0)
        else:
            multiply_half(*arg)

    got[me] = part[0]
    others = got.at[pl.ds(0, GROUPS * GROUPS - 1)]
    r_all = remote(others, others, r_send.at[0], r_recv.at[0], partner)
    r_all.wait_recv()
    scale = 1.0 / math.sqrt(LEN * rows * width * GROUPS)
    out_ref[...] = jnp.sum(got[...], axis=0)[:seqs, :total] * scale

    r_all.wait_send()
    c_copy.wait_send()
    for i in range(GROUPS):
        if i:
            a_copy(i).wait_send()
            q_copy(i).wait_send()
        z_copy(i).wait_send()
        if i in EARLY:
            for dy in (1, -1, 2):
                e_copy(i, dy).wait_send()
        for col in (0, 1):
            if (i, col) in f_way:
                y_copy(i, col, 0).wait_send()
                y_copy(i, col, 1).wait_send()
                f_copy(i, col).wait_send()


def local(adapter_inputs, out_grads, routes, input_eigen_basis, output_eigen_basis, eigen_values, query_grads):
    tokens, rank = adapter_inputs.shape
    experts = input_eigen_basis.shape[0]
    rows = experts * rank
    width = out_grads.shape[1]
    queries = query_grads.shape[0]
    seqs = tokens // LEN
    blk = rows // GROUPS
    dims = (seqs, rows, rank, experts, width, queries, blk)
    piece = seqs * blk
    total = GROUPS * CORES * queries
    vmem, hbm = pl.BlockSpec(memory_space=pltpu.VMEM), pl.BlockSpec(memory_space=pl.ANY)
    dma = pltpu.SemaphoreType.DMA
    return pl.pallas_call(
        functools.partial(kernel, dims),
        out_shape=jax.ShapeDtypeStruct((seqs, total), F32),
        in_specs=[vmem, vmem, vmem, hbm, hbm, hbm, hbm],
        out_specs=vmem,
        scratch_shapes=[
            pltpu.VMEM((seqs, LEN, width), BF16),
            pltpu.VMEM((GROUPS, width, width), BF16),
            pltpu.VMEM((blk, width), F32),
            pltpu.VMEM((GROUPS, piece, width), BF16),
            pltpu.VMEM((GROUPS, GROUPS, piece, width), BF16),
            pltpu.VMEM((GROUPS, CORES, queries, blk, width), BF16),
            pltpu.VMEM((width // LANES, total * blk, LANES), F32),
            pltpu.VMEM((blk, total, width), BF16),
            pltpu.VMEM((width // LANES, GROUPS * piece + blk * 4, LANES), F32),
            pltpu.VMEM((GROUPS, 4, LANES), F32),
            pltpu.VMEM((GROUPS * GROUPS, 4, LANES), F32),
            dma((seqs,)), dma((GROUPS,)), dma((2,)),
            dma((GROUPS,)), dma((GROUPS,)), dma((GROUPS,)), dma((GROUPS,)),
            dma((len(EARLY), YS)), dma((len(EARLY), YS)),
            dma((2, 2, GROUPS)), dma((2, 2, GROUPS)), dma((2, GROUPS)), dma((2, GROUPS)),
            dma((GROUPS,)), dma((GROUPS,)), dma((1,)), dma((1,)), dma((1,)), dma((1,)),
        ],
        compiler_params=pltpu.CompilerParams(
            collective_id=0, has_side_effects=True, vmem_limit_bytes=58 * 2**20
        ),
    )(
        adapter_inputs.T,
        routes.reshape(seqs, 1, LEN),
        input_eigen_basis,
        out_grads.reshape(seqs, LEN, width),
        output_eigen_basis.reshape(GROUPS, width, width),
        eigen_values.reshape(rows, width),
        query_grads.reshape(queries, rows, width),
    )


def solution(mesh):
    placed = (
        P("dp", None),
        P("dp", "mp"),
        P("dp"),
        P(),
        P(None, "mp"),
        P(None, None, "mp"),
        P("dp", None, None, "mp"),
    )
    return jax.shard_map(
        local, mesh=mesh, in_specs=placed, out_specs=P("dp", None), check_vma=False
    )
```

```python
import functools
import math

import jax
import jax.numpy as jnp
from jax import lax
from jax.experimental import pallas as pl
from jax.experimental.pallas import tpu as pltpu
from jax.sharding import PartitionSpec as P

LEN = 1024
LANES = 128
DAMPING = 0.1
F32, BF16 = jnp.float32, jnp.bfloat16

GROUPS = 8
CORES = 2
YS = 4
ORDER = (0, 2, 6, 4, 1, 7, 3, 5)
EARLY = (1, 7)
HALF = 4
SECOND_WAY = {0: 0, 2: 1, 3: 1, 4: 1, 5: 0, 6: 0}
STEPS = (
    ("F", 0, 0), ("Z", 0), ("A", 1), ("A", 2), ("A", 6), ("A", 7), ("Z", 1), ("A", 3), ("F", 0, 1), ("A", 4),
    ("F", 1, 0), ("A", 5), ("Q", 1), ("Q", 7), ("Q", 4), ("Q", 3), ("Q", 5), ("Q", 6), ("Q", 2), ("F", 2, 0),
    ("E", 2, 1), ("Z", 6), ("E", 2, 0), ("Z", 7), ("F", 6, 0), ("Z", 3), ("F", 7, 0), ("F", 1, 1), ("F", 3, 0),
    ("F", 4, 0), ("Z", 4), ("M", 1, 0, 0), ("M", 0, 0, 0), ("E", 5, 1), ("F", 5, 0), ("E", 5, 0), ("M", 0, 1, 0),
    ("M", 0, 2, 0), ("G", 2), ("F", 6, 1), ("M", 1, 1, 0), ("M", 1, 2, 0), ("F", 7, 1), ("C", 0), ("C", 1), ("C", 7),
    ("C", 4), ("C", 3), ("C", 5), ("C", 6), ("C", 2), ("M", 1, 0, 1), ("M", 0, 0, 1), ("R", 0), ("R", 1), ("R", 7),
    ("R", 4), ("F", 3, 1), ("M", 1, 3, 0), ("M", 0, 3, 0), ("R", 3), ("R", 5), ("R", 6), ("R", 2), ("M", 0, 1, 1),
    ("M", 0, 2, 1), ("G", 5), ("F", 4, 1), ("M", 1, 1, 1), ("M", 1, 2, 1), ("M", 1, 3, 1), ("S", 1), ("M", 0, 3, 1),
    ("S", 0),
)
NT = (((1,), (1,)), ((), ()))


def kernel(
    dims,
    a_ref, routes_ref, basis_ref, g_hbm, u_hbm, eig_hbm, q_hbm,
    out_ref,
    g_v, u_v, eig_v, raw, gat, qbuf, qwide, qrow, acc, part, got,
    g_sem, u_sem, l_sem,
    a_send, a_recv, z_send, z_recv, e_send, e_recv, y_send, y_recv, f_send, f_recv,
    q_send, q_recv, c_send, c_recv, r_send, r_recv,
):
    seqs, rows, rank, experts, width, queries, blk = dims
    piece = seqs * blk
    dp, mp = lax.axis_index("dp"), lax.axis_index("mp")
    s, k = dp // CORES, dp % CORES
    y, l = mp // 2, mp % 2

    def dp_peer(b):
        return {"dp": b * CORES + k, "mp": mp}

    def mp_peer(m):
        return {"dp": dp, "mp": m}

    def at(dy, dl):
        return ((y + dy) % YS) * 2 + (l + dl) % 2

    def remote(src, dst, send, recv, dev):
        return pltpu.make_async_remote_copy(
            src_ref=src, dst_ref=dst, send_sem=send, recv_sem=recv, device_id=dev
        )

    partner = {"dp": s * CORES + 1 - k, "mp": mp}

    for n in range(seqs):
        pltpu.make_async_copy(g_hbm.at[n], g_v.at[n], g_sem.at[n]).start()
    eig_copy = pltpu.make_async_copy(
        eig_hbm.at[pl.ds(pl.multiple_of(s * blk, blk), blk), :], eig_v, l_sem.at[0]
    )
    eig_copy.start()

    barrier = pltpu.get_barrier_semaphore()
    greeted = [dp_peer((s + o) % GROUPS) for o in range(1, GROUPS)]
    greeted += [
        {"dp": (s + o) % GROUPS * CORES + k, "mp": at(0, 1)} for o in range(1, GROUPS, 2)
    ]
    greeted += [mp_peer(at(1, 0)), mp_peer(at(YS - 1, 0)), mp_peer(at(0, 1)), partner]
    for device in greeted:
        pl.semaphore_signal(barrier, inc=1, device_id=device)

    basis = jnp.concatenate([basis_ref[e] for e in range(experts)], axis=1).T
    parts, rest = [], basis
    for _ in range(3):
        parts.append(rest.astype(BF16))
        rest = rest - parts[-1].astype(F32)
    row_expert = lax.broadcasted_iota(jnp.int32, (rows, 1), 0) // rank

    def sequence(n):
        pltpu.make_async_copy(g_hbm.at[n], g_v.at[n], g_sem.at[n]).wait()
        a = a_ref[:, n * LEN : (n + 1) * LEN]
        spread = jnp.dot(parts[2], a, preferred_element_type=F32)
        spread += jnp.dot(parts[1], a, preferred_element_type=F32)
        spread += jnp.dot(parts[0], a, preferred_element_type=F32)
        rotated = jnp.where(routes_ref[n] == row_expert, spread, 0.0).astype(BF16)
        sums = jnp.dot(rotated, g_v[n], preferred_element_type=F32).astype(BF16)
        raw[:, n * blk : (n + 1) * blk, :] = sums.reshape(GROUPS, blk, width)

    first_col = [o % 2 for o in ORDER]
    direct = [i for i in range(GROUPS) if i not in EARLY]
    f_way = {(i, first_col[i]): (i + i // HALF) % 2 for i in range(GROUPS)}
    f_way.update({(i, 1 - first_col[i]): SECOND_WAY[i] for i in direct})

    def slot(dy, col, i):
        return gat.at[at(dy % YS, col), i]

    def a_copy(i, low=0, high=seqs):
        b = (s + ORDER[i]) % GROUPS
        device = {"dp": b * CORES + k, "mp": at(0, first_col[i])}
        own = pl.ds(low * blk, (high - low) * blk)
        return remote(raw.at[b, own], gat.at[mp, i, own], a_send.at[i], a_recv.at[i], device)

    def a_landed(i):
        here = slot(0, first_col[i], i)
        return remote(here, here, a_send.at[i], a_recv.at[i], partner)

    def z_copy(i, low=0, high=seqs):
        here = slot(0, first_col[i], i).at[pl.ds(low * blk, (high - low) * blk)]
        return remote(here, here, z_send.at[i], z_recv.at[i], mp_peer(at(0, 1)))

    def z_landed(i):
        here = slot(0, 1 - first_col[i], i)
        return remote(here, here, z_send.at[i], z_recv.at[i], mp_peer(at(0, 1)))

    def way_peer(way):
        return mp_peer(at(1 if way == 0 else YS - 1, 0))

    def y_copy(i, col, way, low=0, high=seqs):
        here = slot(0, col, i).at[pl.ds(low * blk, (high - low) * blk)]
        return remote(here, here, y_send.at[col, way, i], y_recv.at[col, way, i], way_peer(way))

    def y_landed(i, col, way):
        here = slot(-1 if way == 0 else 1, col, i)
        return remote(here, here, y_send.at[col, way, i], y_recv.at[col, way, i], way_peer(way))

    def f_copy(i, col):
        way = f_way[i, col]
        here = slot(-1 if way == 0 else 1, col, i)
        return remote(here, here, f_send.at[col, i], f_recv.at[col, i], way_peer(way))

    def f_landed(i, col):
        here = slot(2, col, i)
        return remote(here, here, f_send.at[col, i], f_recv.at[col, i], partner)

    def e_copy(i, dy):
        here = slot(dy, first_col[i], i)
        n = EARLY.index(i)
        return remote(here, here, e_send.at[n, dy % YS], e_recv.at[n, dy % YS], mp_peer(at(0, 1)))

    def e_landed(i, dy):
        here = slot(dy, 1 - first_col[i], i)
        n = EARLY.index(i)
        return remote(here, here, e_send.at[n, dy % YS], e_recv.at[n, dy % YS], partner)

    def q_source(b):
        return q_hbm.at[:, pl.ds(pl.multiple_of(b * blk, blk), blk), :]

    def q_copy(i):
        b = (s + ORDER[i]) % GROUPS
        return remote(q_source(b), qbuf.at[s, k], q_send.at[i], q_recv.at[i], dp_peer(b))

    def q_landed(i):
        here = qbuf.at[(s + GROUPS - ORDER[i]) % GROUPS, k]
        return remote(here, here, q_send.at[i], q_recv.at[i], partner)

    def both_ways(i, col):
        y_copy(i, col, 0).start()
        y_copy(i, col, 1).start()

    def forward(i, col):
        y_landed(i, col, f_way[i, col]).wait_recv()
        f_copy(i, col).start()

    def other_way(i, col):
        y_landed(i, col, 1 - f_way[i, col]).wait_recv()

    def multiply(m, low, high, first):
        product = jnp.dot(
            gat[m, low:high].reshape((high - low) * piece, width), u_v[m], preferred_element_type=F32
        )
        own = slice(low * piece, high * piece)
        for lanes in range(width // LANES):
            term = product[:, lanes * LANES : (lanes + 1) * LANES]
            acc[lanes, own] = term if first else acc[lanes, own] + term

    for n in range(seqs):
        sequence(n)
        if n == 0:
            pl.semaphore_wait(barrier, len(greeted))
        for i in range(1, GROUPS):
            a_copy(i, n, n + 1).start()
        gat[mp, 0, n * blk : (n + 1) * blk] = raw[s, n * blk : (n + 1) * blk]
        y_copy(0, first_col[0], 0, n, n + 1).start()
        y_copy(0, first_col[0], 1, n, n + 1).start()
        z_copy(0, n, n + 1).start()
    q_own = pltpu.make_async_copy(q_source(s), qbuf.at[s, k], l_sem.at[1])
    q_own.start()
    for m in range(GROUPS):
        pltpu.make_async_copy(u_hbm.at[m], u_v.at[m], u_sem.at[m]).start()
    acc[:, GROUPS * piece :] = jnp.zeros((width // LANES, blk * 4, LANES), F32)
    part[...] = jnp.zeros(part.shape, F32)
    qwide[...] = jnp.zeros(qwide.shape, F32)
    eig_copy.wait()
    eig_v[...] = 1.0 / (eig_v[...] + DAMPING)

    def c_copy(i):
        here = qbuf.at[(s + GROUPS - ORDER[i]) % GROUPS, k]
        return remote(here, here, c_send.at[i], c_recv.at[i], partner)

    def c_landed(i):
        here = qbuf.at[(s + GROUPS - ORDER[i]) % GROUPS, 1 - k]
        return remote(here, here, c_send.at[i], c_recv.at[i], partner)

    total = GROUPS * CORES * queries

    def put_together(i):
        source = (s + GROUPS - ORDER[i]) % GROUPS
        lines = queries * blk
        for lanes in range(width // LANES):
            for core in range(CORES):
                cols = qbuf[source, core, :, :, lanes * LANES : (lanes + 1) * LANES]
                qwide[lanes, core * LANES : core * LANES + lines] = cols.reshape(lines, LANES).astype(F32)
        place = pl.ds(pl.multiple_of(source * blk, blk), blk)

        def one_row(r, carry):
            for lanes in range(width // LANES):
                cols = qwide[lanes, pl.ds(r, blk, stride=blk), :]
                qrow[r, place, lanes * LANES : (lanes + 1) * LANES] = cols.astype(BF16)
            return carry

        lax.fori_loop(0, blk, one_row, 0)

    def score(low, high):
        padded, step = 16, 8

        def some_rows(g, scores):
            for r in [g * step + n for n in range(step)]:
                own = pl.ds(low * piece + r, padded, stride=blk)
                train = jnp.concatenate([acc[lanes, own, :] for lanes in range(width // LANES)], axis=1)
                train = train.astype(BF16).astype(F32) * eig_v[pl.ds(r, 1), :]
                upper = train.astype(BF16).astype(F32)
                both = jnp.concatenate([upper, train - upper], axis=0).astype(BF16)
                scores += lax.dot_general(both, qrow[r], NT, preferred_element_type=F32)
            return scores

        scores = lax.fori_loop(0, blk // step, some_rows, jnp.zeros((2 * padded, LANES), F32))
        scores = scores[:padded] + scores[padded:]
        for i in range(low, high):
            part[i, :seqs] = scores[(i - low) * seqs : (i - low + 1) * seqs]

    me = s * GROUPS + mp

    def r_copy(i, m):
        device = {"dp": (s + GROUPS - ORDER[i]) % GROUPS * CORES + k, "mp": m}
        return remote(part.at[i], got.at[me], r_send.at[0], r_recv.at[0], device)

    def send_scores(low, high):
        for o in (4, 5, 3, 2, 6, 1, 7, 0):
            for i in range(high - 1, low - 1, -1):
                if i or o:
                    r_copy(i, (mp + o) % GROUPS).start()

    waited, loaded, begun = set(), set(), set()

    def wait(copy, *name):
        if name not in waited:
            waited.add(name)
            copy(*name[1:]).wait_recv()

    def y_wait(i, second, way):
        wait(lambda *_: y_landed(i, first_col[i] ^ second, way), "y", i, second, way)

    def multiply_half(part_of, source, second):
        low, high = (0, HALF) if part_of == 0 else (HALF, GROUPS)
        dy = (0, -1, 1, 2)[source]
        for i in range(low, high):
            if source == 0 and not second:
                if i:
                    wait(a_landed, "a", i)
            elif source == 0:
                wait(z_landed, "z", i)
            elif second and i in EARLY:
                e_landed(i, dy).wait_recv()
            elif source == 3:
                wait(lambda *_: f_landed(i, first_col[i] ^ second), "f", i, second)
            else:
                y_wait(i, second, source - 1)
        m, name = at(dy % YS, part_of ^ second), (dy, part_of ^ second)
        if name not in loaded:
            loaded.add(name)
            pltpu.make_async_copy(u_hbm.at[m], u_v.at[m], u_sem.at[m]).wait()
        multiply(m, low, high, part_of not in begun)
        begun.add(part_of)

    for step, *arg in STEPS:
        if step in "AZFEGQCR":
            arg = [ORDER.index(arg[0])] + arg[1:]
        if step == "A":
            wait(a_landed, "a", arg[0])
            both_ways(arg[0], first_col[arg[0]])
            z_copy(arg[0]).start()
        elif step == "Z":
            wait(z_landed, "z", arg[0])
            both_ways(arg[0], 1 - first_col[arg[0]])
        elif step == "F":
            i, second = arg
            y_wait(i, second, f_way[i, first_col[i] ^ second])
            f_copy(i, first_col[i] ^ second).start()
        elif step == "E":
            i, way = arg
            y_wait(i, 0, way)
            e_copy(i, -1 if way == 0 else 1).start()
        elif step == "G":
            i = arg[0]
            wait(lambda *_: f_landed(i, first_col[i]), "f", i, 0)
            e_copy(i, 2).start()
        elif step == "Q":
            q_copy(arg[0]).start()
        elif step == "C":
            i = arg[0]
            if i:
                q_landed(i).wait_recv()
            else:
                q_own.wait()
            c_copy(i).start()
        elif step == "R":
            c_landed(arg[0]).wait_recv()
            put_together(arg[0])
        elif step == "M":
            multiply_half(*arg)
        else:
            low, high = (0, HALF) if arg[0] == 0 else (HALF, GROUPS)
            score(low, high)
            send_scores(low, high)

    got[me] = part[0]
    others = got.at[pl.ds(0, GROUPS * GROUPS - 1)]
    r_all = remote(others, others, r_send.at[0], r_recv.at[0], partner)
    r_all.wait_recv()
    scale = 1.0 / math.sqrt(LEN * rows * width * GROUPS)
    lines = jnp.concatenate([jnp.sum(got[...], axis=0)] * 2, axis=0)
    line = lax.broadcasted_iota(jnp.int32, (LANES, total), 0)
    query = lax.broadcasted_iota(jnp.int32, (LANES, total), 1)
    wanted = query // queries * 8 + query % queries
    chosen = jnp.where(line == wanted, 1.0, 0.0).astype(F32)
    picked = jnp.dot(lines, chosen, precision=lax.Precision.HIGHEST, preferred_element_type=F32)
    out_ref[...] = picked[:seqs] * scale

    r_all.wait_send()
    for i in range(GROUPS):
        if i:
            a_copy(i).wait_send()
            q_copy(i).wait_send()
        z_copy(i).wait_send()
        c_copy(i).wait_send()
        if i in EARLY:
            for dy in (1, -1, 2):
                e_copy(i, dy).wait_send()
        for col in (0, 1):
            if (i, col) in f_way:
                y_copy(i, col, 0).wait_send()
                y_copy(i, col, 1).wait_send()
                f_copy(i, col).wait_send()


def local(adapter_inputs, out_grads, routes, input_eigen_basis, output_eigen_basis, eigen_values, query_grads):
    tokens, rank = adapter_inputs.shape
    experts = input_eigen_basis.shape[0]
    rows = experts * rank
    width = out_grads.shape[1]
    queries = query_grads.shape[0]
    seqs = tokens // LEN
    blk = rows // GROUPS
    dims = (seqs, rows, rank, experts, width, queries, blk)
    piece = seqs * blk
    total = GROUPS * CORES * queries
    vmem, hbm = pl.BlockSpec(memory_space=pltpu.VMEM), pl.BlockSpec(memory_space=pl.ANY)
    dma = pltpu.SemaphoreType.DMA
    return pl.pallas_call(
        functools.partial(kernel, dims),
        out_shape=jax.ShapeDtypeStruct((seqs, total), F32),
        in_specs=[vmem, vmem, vmem, hbm, hbm, hbm, hbm],
        out_specs=vmem,
        scratch_shapes=[
            pltpu.VMEM((seqs, LEN, width), BF16),
            pltpu.VMEM((GROUPS, width, width), BF16),
            pltpu.VMEM((blk, width), F32),
            pltpu.VMEM((GROUPS, piece, width), BF16),
            pltpu.VMEM((GROUPS, GROUPS, piece, width), BF16),
            pltpu.VMEM((GROUPS, CORES, queries, blk, width), BF16),
            pltpu.VMEM((width // LANES, CORES * LANES, LANES), F32),
            pltpu.VMEM((blk, LANES, width), BF16),
            pltpu.VMEM((width // LANES, GROUPS * piece + blk * 4, LANES), F32),
            pltpu.VMEM((GROUPS, 4, LANES), F32),
            pltpu.VMEM((GROUPS * GROUPS, 4, LANES), F32),
            dma((seqs,)), dma((GROUPS,)), dma((2,)),
            dma((GROUPS,)), dma((GROUPS,)), dma((GROUPS,)), dma((GROUPS,)),
            dma((len(EARLY), YS)), dma((len(EARLY), YS)),
            dma((2, 2, GROUPS)), dma((2, 2, GROUPS)), dma((2, GROUPS)), dma((2, GROUPS)),
            dma((GROUPS,)), dma((GROUPS,)), dma((GROUPS,)), dma((GROUPS,)), dma((1,)), dma((1,)),
        ],
        compiler_params=pltpu.CompilerParams(
            collective_id=0, has_side_effects=True, vmem_limit_bytes=58 * 2**20
        ),
    )(
        adapter_inputs.T,
        routes.reshape(seqs, 1, LEN),
        input_eigen_basis,
        out_grads.reshape(seqs, LEN, width),
        output_eigen_basis.reshape(GROUPS, width, width),
        eigen_values.reshape(rows, width),
        query_grads.reshape(queries, rows, width),
    )


def solution(mesh):
    placed = (
        P("dp", None),
        P("dp", "mp"),
        P("dp"),
        P(),
        P(None, "mp"),
        P(None, None, "mp"),
        P("dp", None, None, "mp"),
    )
    return jax.shard_map(
        local, mesh=mesh, in_specs=placed, out_specs=P("dp", None), check_vma=False
    )
```

```python
import functools
import math

import jax
import jax.numpy as jnp
from jax import lax
from jax.experimental import pallas as pl
from jax.experimental.pallas import tpu as pltpu
from jax.sharding import PartitionSpec as P

LEN = 1024
LANES = 128
DAMPING = 0.1
F32, BF16 = jnp.float32, jnp.bfloat16

GROUPS = 8
CORES = 2
YS = 4
ORDER = (0, 2, 6, 4, 1, 7, 3, 5)
EARLY = (1, 7)
HALF = 4
SECOND_WAY = {0: 0, 2: 1, 3: 1, 4: 1, 5: 0, 6: 0}
STEPS = (
    ("F", 0, 0), ("Z", 0), ("A", 1), ("A", 2), ("A", 6), ("A", 7), ("Z", 1), ("A", 3), ("F", 0, 1), ("A", 4),
    ("F", 1, 0), ("A", 5), ("Q", 1), ("Q", 7), ("Q", 4), ("Q", 3), ("Q", 5), ("Q", 6), ("Q", 2), ("F", 2, 0),
    ("E", 2, 1), ("Z", 6), ("E", 2, 0), ("Z", 7), ("F", 6, 0), ("Z", 3), ("F", 7, 0), ("F", 1, 1), ("F", 3, 0),
    ("F", 4, 0), ("Z", 4), ("M", 1, 0, 0), ("M", 0, 0, 0), ("E", 5, 1), ("F", 5, 0), ("E", 5, 0), ("M", 0, 1, 0),
    ("M", 0, 2, 0), ("G", 2), ("F", 6, 1), ("M", 1, 1, 0), ("M", 1, 2, 0), ("F", 7, 1), ("C", 0), ("C", 1), ("C", 7),
    ("C", 4), ("C", 3), ("C", 5), ("C", 6), ("C", 2), ("M", 1, 0, 1), ("M", 0, 0, 1), ("R", 0), ("R", 1), ("R", 7),
    ("R", 4), ("F", 3, 1), ("M", 1, 3, 0), ("M", 0, 3, 0), ("R", 3), ("R", 5), ("R", 6), ("R", 2), ("G", 5),
    ("M", 0, 1, 1), ("M", 0, 2, 1), ("F", 4, 1), ("M", 1, 1, 1), ("M", 1, 2, 1), ("M", 1, 3, 1), ("S", 1),
    ("M", 0, 3, 1), ("S", 0),
)
NT = (((1,), (1,)), ((), ()))


def kernel(
    dims,
    a_ref, routes_ref, basis_ref, g_hbm, u_hbm, eig_hbm, q_hbm,
    out_ref,
    g_v, u_v, eig_v, raw, gat, qbuf, qwide, qrow, acc, part, got,
    g_sem, u_sem, l_sem,
    a_send, a_recv, z_send, z_recv, e_send, e_recv, y_send, y_recv, f_send, f_recv,
    q_send, q_recv, c_send, c_recv, r_send, r_recv,
):
    seqs, rows, rank, experts, width, queries, blk = dims
    piece = seqs * blk
    dp, mp = lax.axis_index("dp"), lax.axis_index("mp")
    s, k = dp // CORES, dp % CORES
    y, l = mp // 2, mp % 2

    def dp_peer(b):
        return {"dp": b * CORES + k, "mp": mp}

    def mp_peer(m):
        return {"dp": dp, "mp": m}

    def at(dy, dl):
        return ((y + dy) % YS) * 2 + (l + dl) % 2

    def remote(src, dst, send, recv, dev):
        return pltpu.make_async_remote_copy(
            src_ref=src, dst_ref=dst, send_sem=send, recv_sem=recv, device_id=dev
        )

    partner = {"dp": s * CORES + 1 - k, "mp": mp}

    for n in range(seqs):
        pltpu.make_async_copy(g_hbm.at[n], g_v.at[n], g_sem.at[n]).start()
    eig_copy = pltpu.make_async_copy(
        eig_hbm.at[pl.ds(pl.multiple_of(s * blk, blk), blk), :], eig_v, l_sem.at[0]
    )
    eig_copy.start()

    barrier = pltpu.get_barrier_semaphore()
    greeted = [dp_peer((s + o) % GROUPS) for o in range(1, GROUPS)]
    greeted += [
        {"dp": (s + o) % GROUPS * CORES + k, "mp": at(0, 1)} for o in range(1, GROUPS, 2)
    ]
    greeted += [mp_peer(at(1, 0)), mp_peer(at(YS - 1, 0)), mp_peer(at(0, 1)), partner]
    for device in greeted:
        pl.semaphore_signal(barrier, inc=1, device_id=device)

    basis = jnp.concatenate([basis_ref[e] for e in range(experts)], axis=1).T
    parts, rest = [], basis
    for _ in range(3):
        parts.append(rest.astype(BF16))
        rest = rest - parts[-1].astype(F32)
    row_expert = lax.broadcasted_iota(jnp.int32, (rows, 1), 0) // rank

    def sequence(n):
        pltpu.make_async_copy(g_hbm.at[n], g_v.at[n], g_sem.at[n]).wait()
        a = a_ref[:, n * LEN : (n + 1) * LEN]
        spread = jnp.dot(parts[2], a, preferred_element_type=F32)
        spread += jnp.dot(parts[1], a, preferred_element_type=F32)
        spread += jnp.dot(parts[0], a, preferred_element_type=F32)
        rotated = jnp.where(routes_ref[n] == row_expert, spread, 0.0).astype(BF16)
        sums = jnp.dot(rotated, g_v[n], preferred_element_type=F32).astype(BF16)
        raw[:, n * blk : (n + 1) * blk, :] = sums.reshape(GROUPS, blk, width)

    first_col = [o % 2 for o in ORDER]
    direct = [i for i in range(GROUPS) if i not in EARLY]
    f_way = {(i, first_col[i]): (i + i // HALF) % 2 for i in range(GROUPS)}
    f_way.update({(i, 1 - first_col[i]): SECOND_WAY[i] for i in direct})

    def slot(dy, col, i):
        return gat.at[at(dy % YS, col), i]

    def a_copy(i, low=0, high=seqs):
        b = (s + ORDER[i]) % GROUPS
        device = {"dp": b * CORES + k, "mp": at(0, first_col[i])}
        own = pl.ds(low * blk, (high - low) * blk)
        return remote(raw.at[b, own], gat.at[mp, i, own], a_send.at[i], a_recv.at[i], device)

    def a_landed(i):
        here = slot(0, first_col[i], i)
        return remote(here, here, a_send.at[i], a_recv.at[i], partner)

    def z_copy(i, low=0, high=seqs):
        here = slot(0, first_col[i], i).at[pl.ds(low * blk, (high - low) * blk)]
        return remote(here, here, z_send.at[i], z_recv.at[i], mp_peer(at(0, 1)))

    def z_landed(i):
        here = slot(0, 1 - first_col[i], i)
        return remote(here, here, z_send.at[i], z_recv.at[i], mp_peer(at(0, 1)))

    def way_peer(way):
        return mp_peer(at(1 if way == 0 else YS - 1, 0))

    def y_copy(i, col, way, low=0, high=seqs):
        here = slot(0, col, i).at[pl.ds(low * blk, (high - low) * blk)]
        return remote(here, here, y_send.at[col, way, i], y_recv.at[col, way, i], way_peer(way))

    def y_landed(i, col, way):
        here = slot(-1 if way == 0 else 1, col, i)
        return remote(here, here, y_send.at[col, way, i], y_recv.at[col, way, i], way_peer(way))

    def f_copy(i, col):
        way = f_way[i, col]
        here = slot(-1 if way == 0 else 1, col, i)
        return remote(here, here, f_send.at[col, i], f_recv.at[col, i], way_peer(way))

    def f_landed(i, col):
        here = slot(2, col, i)
        return remote(here, here, f_send.at[col, i], f_recv.at[col, i], partner)

    def e_copy(i, dy):
        here = slot(dy, first_col[i], i)
        n = EARLY.index(i)
        return remote(here, here, e_send.at[n, dy % YS], e_recv.at[n, dy % YS], mp_peer(at(0, 1)))

    def e_landed(i, dy):
        here = slot(dy, 1 - first_col[i], i)
        n = EARLY.index(i)
        return remote(here, here, e_send.at[n, dy % YS], e_recv.at[n, dy % YS], partner)

    def q_source(b):
        return q_hbm.at[:, pl.ds(pl.multiple_of(b * blk, blk), blk), :]

    def q_copy(i):
        b = (s + ORDER[i]) % GROUPS
        return remote(q_source(b), qbuf.at[s, k], q_send.at[i], q_recv.at[i], dp_peer(b))

    def q_landed(i):
        here = qbuf.at[(s + GROUPS - ORDER[i]) % GROUPS, k]
        return remote(here, here, q_send.at[i], q_recv.at[i], partner)

    def both_ways(i, col):
        y_copy(i, col, 0).start()
        y_copy(i, col, 1).start()

    def forward(i, col):
        y_landed(i, col, f_way[i, col]).wait_recv()
        f_copy(i, col).start()

    def other_way(i, col):
        y_landed(i, col, 1 - f_way[i, col]).wait_recv()

    def multiply(m, low, high, first):
        product = jnp.dot(
            gat[m, low:high].reshape((high - low) * piece, width), u_v[m], preferred_element_type=F32
        )
        own = slice(low * piece, high * piece)
        for lanes in range(width // LANES):
            term = product[:, lanes * LANES : (lanes + 1) * LANES]
            acc[lanes, own] = term if first else acc[lanes, own] + term

    for n in range(seqs):
        sequence(n)
        if n == 0:
            pl.semaphore_wait(barrier, len(greeted))
        for i in (4, 5, 1, 2, 6, 7, 3):
            a_copy(i, n, n + 1).start()
        gat[mp, 0, n * blk : (n + 1) * blk] = raw[s, n * blk : (n + 1) * blk]
        y_copy(0, first_col[0], 0, n, n + 1).start()
        y_copy(0, first_col[0], 1, n, n + 1).start()
        z_copy(0, n, n + 1).start()
    q_own = pltpu.make_async_copy(q_source(s), qbuf.at[s, k], l_sem.at[1])
    q_own.start()
    for m in range(GROUPS):
        pltpu.make_async_copy(u_hbm.at[m], u_v.at[m], u_sem.at[m]).start()
    acc[:, GROUPS * piece :] = jnp.zeros((width // LANES, blk * 4, LANES), F32)
    part[...] = jnp.zeros(part.shape, F32)
    qwide[...] = jnp.zeros(qwide.shape, F32)
    eig_copy.wait()
    eig_v[...] = 1.0 / (eig_v[...] + DAMPING)

    def c_copy(i):
        here = qbuf.at[(s + GROUPS - ORDER[i]) % GROUPS, k]
        return remote(here, here, c_send.at[i], c_recv.at[i], partner)

    def c_landed(i):
        here = qbuf.at[(s + GROUPS - ORDER[i]) % GROUPS, 1 - k]
        return remote(here, here, c_send.at[i], c_recv.at[i], partner)

    total = GROUPS * CORES * queries

    def put_together(i):
        source = (s + GROUPS - ORDER[i]) % GROUPS
        lines = queries * blk
        for lanes in range(width // LANES):
            for core in range(CORES):
                cols = qbuf[source, core, :, :, lanes * LANES : (lanes + 1) * LANES]
                qwide[lanes, core * LANES : core * LANES + lines] = cols.reshape(lines, LANES).astype(F32)
        place = pl.ds(pl.multiple_of(source * blk, blk), blk)

        def one_row(r, carry):
            for lanes in range(width // LANES):
                cols = qwide[lanes, pl.ds(r, blk, stride=blk), :]
                qrow[r, place, lanes * LANES : (lanes + 1) * LANES] = cols.astype(BF16)
            return carry

        lax.fori_loop(0, blk, one_row, 0)

    def score(low, high):
        padded, step = 16, 8

        def some_rows(g, scores):
            for r in [g * step + n for n in range(step)]:
                own = pl.ds(low * piece + r, padded, stride=blk)
                train = jnp.concatenate([acc[lanes, own, :] for lanes in range(width // LANES)], axis=1)
                train = train.astype(BF16).astype(F32) * eig_v[pl.ds(r, 1), :]
                upper = train.astype(BF16).astype(F32)
                both = jnp.concatenate([upper, train - upper], axis=0).astype(BF16)
                scores += lax.dot_general(both, qrow[r], NT, preferred_element_type=F32)
            return scores

        scores = lax.fori_loop(0, blk // step, some_rows, jnp.zeros((2 * padded, LANES), F32))
        scores = scores[:padded] + scores[padded:]
        for i in range(low, high):
            part[i, :seqs] = scores[(i - low) * seqs : (i - low + 1) * seqs]

    me = s * GROUPS + mp

    def r_copy(i, m):
        device = {"dp": (s + GROUPS - ORDER[i]) % GROUPS * CORES + k, "mp": m}
        return remote(part.at[i], got.at[me], r_send.at[0], r_recv.at[0], device)

    def send_scores(low, high):
        for o in (4, 5, 3, 2, 6, 1, 7, 0):
            for i in range(high - 1, low - 1, -1):
                if i or o:
                    r_copy(i, (mp + o) % GROUPS).start()

    waited, loaded, begun = set(), set(), set()

    def wait(copy, *name):
        if name not in waited:
            waited.add(name)
            copy(*name[1:]).wait_recv()

    def y_wait(i, second, way):
        wait(lambda *_: y_landed(i, first_col[i] ^ second, way), "y", i, second, way)

    def multiply_half(part_of, source, second):
        low, high = (0, HALF) if part_of == 0 else (HALF, GROUPS)
        dy = (0, -1, 1, 2)[source]
        for i in range(low, high):
            if source == 0 and not second:
                if i:
                    wait(a_landed, "a", i)
            elif source == 0:
                wait(z_landed, "z", i)
            elif second and i in EARLY:
                e_landed(i, dy).wait_recv()
            elif source == 3:
                wait(lambda *_: f_landed(i, first_col[i] ^ second), "f", i, second)
            else:
                y_wait(i, second, source - 1)
        m, name = at(dy % YS, part_of ^ second), (dy, part_of ^ second)
        if name not in loaded:
            loaded.add(name)
            pltpu.make_async_copy(u_hbm.at[m], u_v.at[m], u_sem.at[m]).wait()
        multiply(m, low, high, part_of not in begun)
        begun.add(part_of)

    for step, *arg in STEPS:
        if step in "AZFEGQCR":
            arg = [ORDER.index(arg[0])] + arg[1:]
        if step == "A":
            wait(a_landed, "a", arg[0])
            both_ways(arg[0], first_col[arg[0]])
            z_copy(arg[0]).start()
        elif step == "Z":
            wait(z_landed, "z", arg[0])
            both_ways(arg[0], 1 - first_col[arg[0]])
        elif step == "F":
            i, second = arg
            y_wait(i, second, f_way[i, first_col[i] ^ second])
            f_copy(i, first_col[i] ^ second).start()
        elif step == "E":
            i, way = arg
            y_wait(i, 0, way)
            e_copy(i, -1 if way == 0 else 1).start()
        elif step == "G":
            i = arg[0]
            wait(lambda *_: f_landed(i, first_col[i]), "f", i, 0)
            e_copy(i, 2).start()
        elif step == "Q":
            q_copy(arg[0]).start()
        elif step == "C":
            i = arg[0]
            if i:
                q_landed(i).wait_recv()
            else:
                q_own.wait()
            c_copy(i).start()
        elif step == "R":
            c_landed(arg[0]).wait_recv()
            put_together(arg[0])
        elif step == "M":
            multiply_half(*arg)
        else:
            low, high = (0, HALF) if arg[0] == 0 else (HALF, GROUPS)
            score(low, high)
            send_scores(low, high)

    got[me] = part[0]
    others = got.at[pl.ds(0, GROUPS * GROUPS - 1)]
    r_all = remote(others, others, r_send.at[0], r_recv.at[0], partner)
    r_all.wait_recv()
    scale = 1.0 / math.sqrt(LEN * rows * width * GROUPS)
    lines = jnp.concatenate([jnp.sum(got[...], axis=0)] * 2, axis=0)
    line = lax.broadcasted_iota(jnp.int32, (LANES, total), 0)
    query = lax.broadcasted_iota(jnp.int32, (LANES, total), 1)
    wanted = query // queries * 8 + query % queries
    chosen = jnp.where(line == wanted, 1.0, 0.0).astype(F32)
    picked = jnp.dot(lines, chosen, precision=lax.Precision.HIGHEST, preferred_element_type=F32)
    out_ref[...] = picked[:seqs] * scale

    r_all.wait_send()
    for i in range(GROUPS):
        if i:
            a_copy(i).wait_send()
            q_copy(i).wait_send()
        z_copy(i).wait_send()
        c_copy(i).wait_send()
        if i in EARLY:
            for dy in (1, -1, 2):
                e_copy(i, dy).wait_send()
        for col in (0, 1):
            if (i, col) in f_way:
                y_copy(i, col, 0).wait_send()
                y_copy(i, col, 1).wait_send()
                f_copy(i, col).wait_send()


def local(adapter_inputs, out_grads, routes, input_eigen_basis, output_eigen_basis, eigen_values, query_grads):
    tokens, rank = adapter_inputs.shape
    experts = input_eigen_basis.shape[0]
    rows = experts * rank
    width = out_grads.shape[1]
    queries = query_grads.shape[0]
    seqs = tokens // LEN
    blk = rows // GROUPS
    dims = (seqs, rows, rank, experts, width, queries, blk)
    piece = seqs * blk
    total = GROUPS * CORES * queries
    vmem, hbm = pl.BlockSpec(memory_space=pltpu.VMEM), pl.BlockSpec(memory_space=pl.ANY)
    dma = pltpu.SemaphoreType.DMA
    return pl.pallas_call(
        functools.partial(kernel, dims),
        out_shape=jax.ShapeDtypeStruct((seqs, total), F32),
        in_specs=[vmem, vmem, vmem, hbm, hbm, hbm, hbm],
        out_specs=vmem,
        scratch_shapes=[
            pltpu.VMEM((seqs, LEN, width), BF16),
            pltpu.VMEM((GROUPS, width, width), BF16),
            pltpu.VMEM((blk, width), F32),
            pltpu.VMEM((GROUPS, piece, width), BF16),
            pltpu.VMEM((GROUPS, GROUPS, piece, width), BF16),
            pltpu.VMEM((GROUPS, CORES, queries, blk, width), BF16),
            pltpu.VMEM((width // LANES, CORES * LANES, LANES), F32),
            pltpu.VMEM((blk, LANES, width), BF16),
            pltpu.VMEM((width // LANES, GROUPS * piece + blk * 4, LANES), F32),
            pltpu.VMEM((GROUPS, 4, LANES), F32),
            pltpu.VMEM((GROUPS * GROUPS, 4, LANES), F32),
            dma((seqs,)), dma((GROUPS,)), dma((2,)),
            dma((GROUPS,)), dma((GROUPS,)), dma((GROUPS,)), dma((GROUPS,)),
            dma((len(EARLY), YS)), dma((len(EARLY), YS)),
            dma((2, 2, GROUPS)), dma((2, 2, GROUPS)), dma((2, GROUPS)), dma((2, GROUPS)),
            dma((GROUPS,)), dma((GROUPS,)), dma((GROUPS,)), dma((GROUPS,)), dma((1,)), dma((1,)),
        ],
        compiler_params=pltpu.CompilerParams(
            collective_id=0, has_side_effects=True, vmem_limit_bytes=58 * 2**20
        ),
    )(
        adapter_inputs.T,
        routes.reshape(seqs, 1, LEN),
        input_eigen_basis,
        out_grads.reshape(seqs, LEN, width),
        output_eigen_basis.reshape(GROUPS, width, width),
        eigen_values.reshape(rows, width),
        query_grads.reshape(queries, rows, width),
    )


def solution(mesh):
    placed = (
        P("dp", None),
        P("dp", "mp"),
        P("dp"),
        P(),
        P(None, "mp"),
        P(None, None, "mp"),
        P("dp", None, None, "mp"),
    )
    return jax.shard_map(
        local, mesh=mesh, in_specs=placed, out_specs=P("dp", None), check_vma=False
    )
```

```python
import functools
import math

import jax
import jax.numpy as jnp
from jax import lax
from jax.experimental import pallas as pl
from jax.experimental.pallas import tpu as pltpu
from jax.sharding import PartitionSpec as P

LEN = 1024
LANES = 128
DAMPING = 0.1
F32, BF16 = jnp.float32, jnp.bfloat16

GROUPS = 8
CORES = 2
YS = 4
ORDER = (0, 2, 6, 4, 1, 7, 3, 5)
EARLY = (1, 7)
HALF = 4
SECOND_WAY = {0: 0, 2: 1, 3: 1, 4: 1, 5: 0, 6: 0}
STEPS = (
    ("F", 0, 0), ("Z", 0), ("A", 1), ("A", 2), ("A", 6), ("A", 7), ("Z", 1), ("A", 3), ("F", 0, 1), ("A", 4),
    ("F", 1, 0), ("A", 5), ("Q", 1), ("Q", 7), ("Q", 4), ("Q", 3), ("Q", 5), ("Q", 6), ("Q", 2), ("F", 2, 0),
    ("E", 2, 1), ("Z", 6), ("E", 2, 0), ("Z", 7), ("F", 6, 0), ("Z", 3), ("F", 7, 0), ("F", 1, 1), ("F", 3, 0),
    ("F", 4, 0), ("Z", 4), ("M", 1, 0, 0), ("M", 0, 0, 0), ("E", 5, 1), ("F", 5, 0), ("E", 5, 0), ("M", 0, 1, 0),
    ("M", 0, 2, 0), ("G", 2), ("F", 6, 1), ("M", 1, 1, 0), ("M", 1, 2, 0), ("F", 7, 1), ("C", 0), ("C", 1), ("C", 7),
    ("C", 4), ("C", 3), ("C", 5), ("C", 6), ("C", 2), ("M", 1, 0, 1), ("M", 0, 0, 1), ("R", 0), ("R", 1), ("R", 7),
    ("R", 4), ("F", 3, 1), ("M", 1, 3, 0), ("M", 0, 3, 0), ("R", 3), ("R", 5), ("R", 6), ("R", 2), ("G", 5),
    ("M", 0, 1, 1), ("M", 0, 2, 1), ("F", 4, 1), ("M", 1, 1, 1), ("M", 1, 2, 1), ("M", 1, 3, 1), ("S", 1),
    ("M", 0, 3, 1), ("S", 0),
)
NT = (((1,), (1,)), ((), ()))


def kernel(
    dims,
    a_ref, routes_ref, basis_ref, g_hbm, u_hbm, eig_hbm, q_hbm,
    out_ref,
    g_v, u_v, eig_v, raw, gat, qbuf, qwide, qrow, acc, part, got,
    g_sem, u_sem, l_sem,
    a_send, a_recv, z_send, z_recv, e_send, e_recv, y_send, y_recv, f_send, f_recv,
    q_send, q_recv, c_send, c_recv, r_send, r_recv,
):
    seqs, rows, rank, experts, width, queries, blk = dims
    piece = seqs * blk
    dp, mp = lax.axis_index("dp"), lax.axis_index("mp")
    s, k = dp // CORES, dp % CORES
    y, l = mp // 2, mp % 2

    def dp_peer(b):
        return {"dp": b * CORES + k, "mp": mp}

    def mp_peer(m):
        return {"dp": dp, "mp": m}

    def at(dy, dl):
        return ((y + dy) % YS) * 2 + (l + dl) % 2

    def remote(src, dst, send, recv, dev):
        return pltpu.make_async_remote_copy(
            src_ref=src, dst_ref=dst, send_sem=send, recv_sem=recv, device_id=dev
        )

    partner = {"dp": s * CORES + 1 - k, "mp": mp}

    for n in range(seqs):
        pltpu.make_async_copy(g_hbm.at[n], g_v.at[n], g_sem.at[n]).start()
    eig_copy = pltpu.make_async_copy(
        eig_hbm.at[pl.ds(pl.multiple_of(s * blk, blk), blk), :], eig_v, l_sem.at[0]
    )
    eig_copy.start()

    barrier = pltpu.get_barrier_semaphore()
    greeted = [dp_peer((s + o) % GROUPS) for o in range(1, GROUPS)]
    greeted += [
        {"dp": (s + o) % GROUPS * CORES + k, "mp": at(0, 1)} for o in range(1, GROUPS, 2)
    ]
    greeted += [mp_peer(at(1, 0)), mp_peer(at(YS - 1, 0)), mp_peer(at(0, 1)), partner]
    for device in greeted:
        pl.semaphore_signal(barrier, inc=1, device_id=device)

    basis = jnp.concatenate([basis_ref[e] for e in range(experts)], axis=1).T
    parts, rest = [], basis
    for _ in range(3):
        parts.append(rest.astype(BF16))
        rest = rest - parts[-1].astype(F32)
    row_expert = lax.broadcasted_iota(jnp.int32, (rows, 1), 0) // rank

    def sequence(n):
        pltpu.make_async_copy(g_hbm.at[n], g_v.at[n], g_sem.at[n]).wait()
        a = a_ref[:, n * LEN : (n + 1) * LEN]
        spread = jnp.dot(parts[2], a, preferred_element_type=F32)
        spread += jnp.dot(parts[1], a, preferred_element_type=F32)
        spread += jnp.dot(parts[0], a, preferred_element_type=F32)
        rotated = jnp.where(routes_ref[n] == row_expert, spread, 0.0).astype(BF16)
        sums = jnp.dot(rotated, g_v[n], preferred_element_type=F32).astype(BF16)
        raw[:, n * blk : (n + 1) * blk, :] = sums.reshape(GROUPS, blk, width)

    first_col = [o % 2 for o in ORDER]
    direct = [i for i in range(GROUPS) if i not in EARLY]
    f_way = {(i, first_col[i]): (i + i // HALF) % 2 for i in range(GROUPS)}
    f_way.update({(i, 1 - first_col[i]): SECOND_WAY[i] for i in direct})

    def slot(dy, col, i):
        return gat.at[at(dy % YS, col), i]

    def a_copy(i, low=0, high=seqs):
        b = (s + ORDER[i]) % GROUPS
        device = {"dp": b * CORES + k, "mp": at(0, first_col[i])}
        own = pl.ds(low * blk, (high - low) * blk)
        return remote(raw.at[b, own], gat.at[mp, i, own], a_send.at[i], a_recv.at[i], device)

    def a_landed(i):
        here = slot(0, first_col[i], i)
        return remote(here, here, a_send.at[i], a_recv.at[i], partner)

    def z_copy(i, low=0, high=seqs):
        here = slot(0, first_col[i], i).at[pl.ds(low * blk, (high - low) * blk)]
        return remote(here, here, z_send.at[i], z_recv.at[i], mp_peer(at(0, 1)))

    def z_landed(i):
        here = slot(0, 1 - first_col[i], i)
        return remote(here, here, z_send.at[i], z_recv.at[i], mp_peer(at(0, 1)))

    def way_peer(way):
        return mp_peer(at(1 if way == 0 else YS - 1, 0))

    def y_copy(i, col, way, low=0, high=seqs):
        here = slot(0, col, i).at[pl.ds(low * blk, (high - low) * blk)]
        return remote(here, here, y_send.at[col, way, i], y_recv.at[col, way, i], way_peer(way))

    def y_landed(i, col, way):
        here = slot(-1 if way == 0 else 1, col, i)
        return remote(here, here, y_send.at[col, way, i], y_recv.at[col, way, i], way_peer(way))

    def f_copy(i, col):
        way = f_way[i, col]
        here = slot(-1 if way == 0 else 1, col, i)
        return remote(here, here, f_send.at[col, i], f_recv.at[col, i], way_peer(way))

    def f_landed(i, col):
        here = slot(2, col, i)
        return remote(here, here, f_send.at[col, i], f_recv.at[col, i], partner)

    def e_copy(i, dy):
        here = slot(dy, first_col[i], i)
        n = EARLY.index(i)
        return remote(here, here, e_send.at[n, dy % YS], e_recv.at[n, dy % YS], mp_peer(at(0, 1)))

    def e_landed(i, dy):
        here = slot(dy, 1 - first_col[i], i)
        n = EARLY.index(i)
        return remote(here, here, e_send.at[n, dy % YS], e_recv.at[n, dy % YS], partner)

    def q_source(b):
        return q_hbm.at[:, pl.ds(pl.multiple_of(b * blk, blk), blk), :]

    def q_copy(i):
        b = (s + ORDER[i]) % GROUPS
        return remote(q_source(b), qbuf.at[s, k], q_send.at[i], q_recv.at[i], dp_peer(b))

    def q_landed(i):
        here = qbuf.at[(s + GROUPS - ORDER[i]) % GROUPS, k]
        return remote(here, here, q_send.at[i], q_recv.at[i], partner)

    def both_ways(i, col):
        y_copy(i, col, 0).start()
        y_copy(i, col, 1).start()

    def forward(i, col):
        y_landed(i, col, f_way[i, col]).wait_recv()
        f_copy(i, col).start()

    def other_way(i, col):
        y_landed(i, col, 1 - f_way[i, col]).wait_recv()

    def multiply(m, low, high, first):
        product = jnp.dot(
            gat[m, low:high].reshape((high - low) * piece, width), u_v[m], preferred_element_type=F32
        )
        own = slice(low * piece, high * piece)
        for lanes in range(width // LANES):
            term = product[:, lanes * LANES : (lanes + 1) * LANES]
            acc[lanes, own] = term if first else acc[lanes, own] + term

    for n in range(seqs):
        sequence(n)
        if n == 0:
            pl.semaphore_wait(barrier, len(greeted))
        for i in (4, 5, 1, 2, 6, 7, 3):
            a_copy(i, n, n + 1).start()
        gat[mp, 0, n * blk : (n + 1) * blk] = raw[s, n * blk : (n + 1) * blk]
        y_copy(0, first_col[0], 0, n, n + 1).start()
        y_copy(0, first_col[0], 1, n, n + 1).start()
        z_copy(0, n, n + 1).start()
    q_own = pltpu.make_async_copy(q_source(s), qbuf.at[s, k], l_sem.at[1])
    q_own.start()
    for m in range(GROUPS):
        pltpu.make_async_copy(u_hbm.at[m], u_v.at[m], u_sem.at[m]).start()
    acc[:, GROUPS * piece :] = jnp.zeros((width // LANES, blk * 5, LANES), F32)
    part[...] = jnp.zeros(part.shape, F32)
    qwide[...] = jnp.zeros(qwide.shape, F32)
    eig_copy.wait()
    eig_v[...] = 1.0 / (eig_v[...] + DAMPING)

    def c_copy(i):
        here = qbuf.at[(s + GROUPS - ORDER[i]) % GROUPS, k]
        return remote(here, here, c_send.at[i], c_recv.at[i], partner)

    def c_landed(i):
        here = qbuf.at[(s + GROUPS - ORDER[i]) % GROUPS, 1 - k]
        return remote(here, here, c_send.at[i], c_recv.at[i], partner)

    total = GROUPS * CORES * queries

    def put_together(i):
        source = (s + GROUPS - ORDER[i]) % GROUPS
        lines = queries * blk
        for lanes in range(width // LANES):
            for core in range(CORES):
                cols = qbuf[source, core, :, :, lanes * LANES : (lanes + 1) * LANES]
                qwide[lanes, core * LANES : core * LANES + lines] = cols.reshape(lines, LANES).astype(F32)
        place = pl.ds(pl.multiple_of(source * blk, blk), blk)

        def one_row(r, carry):
            for lanes in range(width // LANES):
                cols = qwide[lanes, pl.ds(r, blk, stride=blk), :]
                qrow[r, place, lanes * LANES : (lanes + 1) * LANES] = cols.astype(BF16)
            return carry

        lax.fori_loop(0, blk, one_row, 0)

    def score(low, high):
        padded, step = 16, 8

        def some_rows(g, scores):
            for r in [g * step + n for n in range(step)]:
                own = pl.ds(low * piece + r, padded, stride=blk)
                train = jnp.concatenate([acc[lanes, own, :] for lanes in range(width // LANES)], axis=1)
                train = train.astype(BF16).astype(F32) * eig_v[pl.ds(r, 1), :]
                upper = train.astype(BF16).astype(F32)
                both = jnp.concatenate([upper, train - upper], axis=0).astype(BF16)
                scores += lax.dot_general(both, qrow[r], NT, preferred_element_type=F32)
            return scores

        scores = lax.fori_loop(0, blk // step, some_rows, jnp.zeros((2 * padded, LANES), F32))
        scores = scores[:padded] + scores[padded:]
        for i in range(low, high):
            part[i, :seqs] = scores[(i - low) * seqs : (i - low + 1) * seqs]

    me = s * GROUPS + mp

    def r_copy(i, m):
        device = {"dp": (s + GROUPS - ORDER[i]) % GROUPS * CORES + k, "mp": m}
        return remote(part.at[i], got.at[me], r_send.at[0], r_recv.at[0], device)

    def send_scores(low, high):
        for o in (4, 5, 3, 2, 6, 1, 7, 0):
            for i in range(high - 1, low - 1, -1):
                if i or o:
                    r_copy(i, (mp + o) % GROUPS).start()

    waited, loaded, begun = set(), set(), set()

    def wait(copy, *name):
        if name not in waited:
            waited.add(name)
            copy(*name[1:]).wait_recv()

    def y_wait(i, second, way):
        wait(lambda *_: y_landed(i, first_col[i] ^ second, way), "y", i, second, way)

    def multiply_half(part_of, source, second):
        low, high = (0, HALF) if part_of == 0 else (HALF, GROUPS)
        dy = (0, -1, 1, 2)[source]
        for i in range(low, high):
            if source == 0 and not second:
                if i:
                    wait(a_landed, "a", i)
            elif source == 0:
                wait(z_landed, "z", i)
            elif second and i in EARLY:
                e_landed(i, dy).wait_recv()
            elif source == 3:
                wait(lambda *_: f_landed(i, first_col[i] ^ second), "f", i, second)
            else:
                y_wait(i, second, source - 1)
        m, name = at(dy % YS, part_of ^ second), (dy, part_of ^ second)
        if name not in loaded:
            loaded.add(name)
            pltpu.make_async_copy(u_hbm.at[m], u_v.at[m], u_sem.at[m]).wait()
        multiply(m, low, high, part_of not in begun)
        begun.add(part_of)

    for step, *arg in STEPS:
        if step in "AZFEGQCR":
            arg = [ORDER.index(arg[0])] + arg[1:]
        if step == "A":
            wait(a_landed, "a", arg[0])
            both_ways(arg[0], first_col[arg[0]])
            z_copy(arg[0]).start()
        elif step == "Z":
            wait(z_landed, "z", arg[0])
            both_ways(arg[0], 1 - first_col[arg[0]])
        elif step == "F":
            i, second = arg
            y_wait(i, second, f_way[i, first_col[i] ^ second])
            f_copy(i, first_col[i] ^ second).start()
        elif step == "E":
            i, way = arg
            y_wait(i, 0, way)
            e_copy(i, -1 if way == 0 else 1).start()
        elif step == "G":
            i = arg[0]
            wait(lambda *_: f_landed(i, first_col[i]), "f", i, 0)
            e_copy(i, 2).start()
        elif step == "Q":
            q_copy(arg[0]).start()
        elif step == "C":
            i = arg[0]
            if i:
                q_landed(i).wait_recv()
            else:
                q_own.wait()
            c_copy(i).start()
        elif step == "R":
            c_landed(arg[0]).wait_recv()
            put_together(arg[0])
        elif step == "M":
            multiply_half(*arg)
        else:
            low, high = (0, HALF) if arg[0] == 0 else (HALF, GROUPS)
            score(low, high)
            send_scores(low, high)

    got[me] = part[0]
    others = got.at[pl.ds(0, GROUPS * GROUPS - 1)]
    r_all = remote(others, others, r_send.at[0], r_recv.at[0], partner)
    r_all.wait_recv()
    scale = 1.0 / math.sqrt(LEN * rows * width * GROUPS)
    lines = jnp.concatenate([jnp.sum(got[...], axis=0)] * 2, axis=0)
    line = lax.broadcasted_iota(jnp.int32, (LANES, total), 0)
    query = lax.broadcasted_iota(jnp.int32, (LANES, total), 1)
    wanted = query // queries * 8 + query % queries
    chosen = jnp.where(line == wanted, 1.0, 0.0).astype(F32)
    picked = jnp.dot(lines, chosen, precision=lax.Precision.HIGHEST, preferred_element_type=F32)
    out_ref[...] = picked[:seqs] * scale

    r_all.wait_send()
    for i in range(GROUPS):
        if i:
            a_copy(i).wait_send()
            q_copy(i).wait_send()
        z_copy(i).wait_send()
        c_copy(i).wait_send()
        if i in EARLY:
            for dy in (1, -1, 2):
                e_copy(i, dy).wait_send()
        for col in (0, 1):
            if (i, col) in f_way:
                y_copy(i, col, 0).wait_send()
                y_copy(i, col, 1).wait_send()
                f_copy(i, col).wait_send()


def local(adapter_inputs, out_grads, routes, input_eigen_basis, output_eigen_basis, eigen_values, query_grads):
    tokens, rank = adapter_inputs.shape
    experts = input_eigen_basis.shape[0]
    rows = experts * rank
    width = out_grads.shape[1]
    queries = query_grads.shape[0]
    seqs = tokens // LEN
    blk = rows // GROUPS
    dims = (seqs, rows, rank, experts, width, queries, blk)
    piece = seqs * blk
    total = GROUPS * CORES * queries
    vmem, hbm = pl.BlockSpec(memory_space=pltpu.VMEM), pl.BlockSpec(memory_space=pl.ANY)
    dma = pltpu.SemaphoreType.DMA
    return pl.pallas_call(
        functools.partial(kernel, dims),
        out_shape=jax.ShapeDtypeStruct((seqs, total), F32),
        in_specs=[vmem, vmem, vmem, hbm, hbm, hbm, hbm],
        out_specs=vmem,
        scratch_shapes=[
            pltpu.VMEM((seqs, LEN, width), BF16),
            pltpu.VMEM((GROUPS, width, width), BF16),
            pltpu.VMEM((blk, width), F32),
            pltpu.VMEM((GROUPS, piece, width), BF16),
            pltpu.VMEM((GROUPS, GROUPS, piece, width), BF16),
            pltpu.VMEM((GROUPS, CORES, queries, blk, width), BF16),
            pltpu.VMEM((width // LANES, CORES * LANES + blk, LANES), F32),
            pltpu.VMEM((blk, LANES, width), BF16),
            pltpu.VMEM((width // LANES, GROUPS * piece + blk * 5, LANES), F32),
            pltpu.VMEM((GROUPS, 4, LANES), F32),
            pltpu.VMEM((GROUPS * GROUPS, 4, LANES), F32),
            dma((seqs,)), dma((GROUPS,)), dma((2,)),
            dma((GROUPS,)), dma((GROUPS,)), dma((GROUPS,)), dma((GROUPS,)),
            dma((len(EARLY), YS)), dma((len(EARLY), YS)),
            dma((2, 2, GROUPS)), dma((2, 2, GROUPS)), dma((2, GROUPS)), dma((2, GROUPS)),
            dma((GROUPS,)), dma((GROUPS,)), dma((GROUPS,)), dma((GROUPS,)), dma((1,)), dma((1,)),
        ],
        compiler_params=pltpu.CompilerParams(
            collective_id=0, has_side_effects=True, vmem_limit_bytes=58 * 2**20
        ),
    )(
        adapter_inputs.T,
        routes.reshape(seqs, 1, LEN),
        input_eigen_basis,
        out_grads.reshape(seqs, LEN, width),
        output_eigen_basis.reshape(GROUPS, width, width),
        eigen_values.reshape(rows, width),
        query_grads.reshape(queries, rows, width),
    )


def solution(mesh):
    placed = (
        P("dp", None),
        P("dp", "mp"),
        P("dp"),
        P(),
        P(None, "mp"),
        P(None, None, "mp"),
        P("dp", None, None, "mp"),
    )
    return jax.shard_map(
        local, mesh=mesh, in_specs=placed, out_specs=P("dp", None), check_vma=False
    )
```
